32 devices in a mesh: ingest: 16 (over z, y, x), codes: 2 (over core).
Axes of the slice: x: 2, y: 2, z: 4, core: 2. Of those that a mesh axis runs over, the one named last changes fastest.
Arguments:
- vectors: bfloat16 [4096, 1024], P('ingest'), may hold values from -6 to 6
- codes: int32 [2, 4096], P(None, 'ingest'), may hold values from 0 to 4095, as said below
- codebook: bfloat16 [2, 4096, 1024], P('codes', 'ingest'), may hold values from -5 to 5
- pairs: int32 [64, 64], replicated, may hold values from 0 to 63, as said below
Outputs:
- new_codebook: float32 [2, 4096, 1024], P('codes', 'ingest')
- gram: float32 [2, 4096, 8192], P('codes', 'ingest')
The draws below stay inside these ranges and needn't reach their ends.
Inputs may be any that keep to these rules, and one draw needn't show every extreme that they name: In each codebook and each aligned block of 256 vectors (the vectors of one index of ingest), at most 32 codes fall in any one range j * 256 to (j + 1) * 256 - 1; in each codebook one such range holds exactly 32 codes of every block. `pairs`: block s is codes (s % 32) * 128 to (s % 32) * 128 + 127 of codebook s // 32; every entry of row r names a block of a codebook other than that of block r; entries may repeat.
All inputs are finite; a program needn't handle non-finite values.
Results may differ from the reference program's by a relative error of at most 0.015.
Values may be sent and summed in bfloat16 or wider, within the bound.
A program may use at most 64 MiB of HBM per device.

```python
import jax
import jax.numpy as jnp
from jax import lax

D = 1024
K = 4096
BLK = 128
P_SIZE = 64
VEC_DEV = 256
M = 2
VECTORS = 4096
OWN = 256
CAP = 32
KB = 32
BLOCKS = 64


def draw_codes(key, part):
    sources = VECTORS // VEC_DEV
    owners = K // OWN
    hot_key, pool_key, order_key, within_key = jax.random.split(key, 4)
    hot_range = jax.random.randint(hot_key, (M, 1, 1), 0, owners).astype(jnp.int32)
    base_pool = jnp.arange((owners - 1) * CAP, dtype=jnp.int32) // CAP

    def shuffle_pool(subkey):
        return jax.random.permutation(subkey, base_pool)

    def shuffle_order(subkey):
        return jax.random.permutation(subkey, jnp.arange(VEC_DEV, dtype=jnp.int32))
    pool_keys = jax.random.split(pool_key, M * sources)
    shuffled = jax.vmap(shuffle_pool)(pool_keys).reshape(M, sources, (owners - 1) * CAP)
    shuffled = shuffled[:, :, :VEC_DEV - CAP]
    others = (hot_range + 1 + shuffled) % owners
    labels = jnp.concatenate([jnp.broadcast_to(hot_range, (M, sources, CAP)), others], axis=2)
    order_keys = jax.random.split(order_key, M * sources)
    order = jax.vmap(shuffle_order)(order_keys).reshape(M, sources, VEC_DEV)
    labels = jnp.take_along_axis(labels, order, axis=2)
    within = jax.random.randint(within_key, (M, sources, VEC_DEV), 0, OWN).astype(jnp.int32)
    return (labels * OWN + within).reshape(M, VECTORS).astype(jnp.int32)


def draw_pairs(key, part):
    book_key, block_key = jax.random.split(key)
    row_books = (jnp.arange(BLOCKS, dtype=jnp.int32) // KB)[:, None]
    book_step = jax.random.randint(book_key, (BLOCKS, P_SIZE), 1, M).astype(jnp.int32)
    partner_book = (row_books + book_step) % M
    partner_block = jax.random.randint(block_key, (BLOCKS, P_SIZE), 0, KB).astype(jnp.int32)
    return (partner_book * KB + partner_block).astype(jnp.int32)


def block_scale(key, dims, pieces, smallest, largest):
    def one(position, blocks):
        draws = jax.random.uniform(jax.random.fold_in(jax.random.fold_in(key, 6), position), (blocks,), jnp.float32, smallest / len(pieces), largest / len(pieces))
        return jnp.repeat(jnp.exp(draws), dims[position] // blocks).reshape((-1,) + (1,) * (len(dims) - position - 1))

    gain = one(*pieces[0])
    for cut in pieces[1:]:
        gain = gain * one(*cut)
    return gain


def centred(rng, dims, deviation, limit, shards=(), held_as=jnp.bfloat16):
    values = deviation * jax.random.normal(rng, dims, jnp.float32)
    if shards:
        values = values * block_scale(rng, dims, shards, -0.22, 0.18)
    return jnp.clip(values, -limit, limit).astype(held_as)


def setup_inputs(seed: int = 0) -> dict:
    arg_keys = jax.random.split(jax.random.key(seed), 5)
    vectors = centred(arg_keys[0], (VECTORS, D), 1.0, 6.0, ((0, 16),))
    codes = draw_codes(jax.random.fold_in(arg_keys[4], 71), 0)
    codebook = centred(arg_keys[2], (M, K, D), 0.35, 5.0, ((0, 2), (1, 16)))
    pairs = draw_pairs(jax.random.fold_in(arg_keys[4], 71), 0)
    return dict(vectors=vectors, codes=codes, codebook=codebook, pairs=pairs)


def reference(vectors, codes, codebook, pairs):
    recon = jnp.zeros((VECTORS, D), jnp.float32)
    for book_index in range(M):
        recon = recon + jnp.take(codebook[book_index], codes[book_index], axis=0).astype(jnp.float32)
    residual = (vectors.astype(jnp.float32) - recon).astype(jnp.bfloat16)
    residual_wide = residual.astype(jnp.float32)
    codes_by_vector = codes.T
    slot_columns = jnp.arange(P_SIZE, dtype=jnp.int32)[None, :] * BLK

    def refit(book_global):
        own_code = lax.dynamic_index_in_dim(codes, book_global, 0, keepdims=False)
        right_side = jax.ops.segment_sum(residual_wide, own_code, num_segments=K)
        code_count = jax.ops.segment_sum(jnp.ones((VECTORS,), jnp.float32), own_code, num_segments=K)
        current = lax.dynamic_index_in_dim(codebook, book_global, 0, keepdims=False).astype(jnp.float32)
        updated = current + (right_side - 2.0 * current) / (code_count[:, None] + 2.0)
        block_id = ((book_global * K + own_code) // BLK).astype(jnp.int32)
        partner = jnp.take(pairs, block_id, axis=0)
        partner_code = jnp.take_along_axis(codes_by_vector, (partner // KB).astype(jnp.int32), axis=1)
        offset = partner_code - (partner % KB) * BLK
        valid = (offset >= 0) & (offset < BLK)
        column = (slot_columns + jnp.clip(offset, 0, BLK - 1)).astype(jnp.int32)
        weight = jnp.where(valid, 1.0, 0.0).astype(jnp.float32)
        gram_book = jnp.zeros((K, P_SIZE * BLK), jnp.float32).at[own_code[:, None], column].add(weight)
        return updated, gram_book

    new_codebook, gram = lax.map(refit, jnp.arange(M, dtype=jnp.int32))
    return new_codebook, gram
```

```python
import functools

import jax
import jax.numpy as jnp
from jax import lax
from jax.experimental import pallas as pl
from jax.experimental.pallas import tpu as pltpu
from jax.sharding import PartitionSpec as P

K = 4096
BLK = 128
P_SIZE = 64
KB = 32
CHUNKS = 2
MESH = pl.DeviceIdType.MESH
VMEM_BYTES = 48 * 1024 * 1024


def whole(ref, sem):
    return pltpu.make_async_copy(ref, ref, sem)


def exchange_kernel(
    n, own, cap,
    codes_ref, vec_ref, book_ref,
    got_ref, table_ref, member_ref,
    allc, picks, ret, send, tabv, memv,
    code_send, code_recv, one_send, one_recv, two_send, two_recv, local_sem, out_sem,
):
    me = lax.axis_index("ingest")
    book = lax.axis_index("codes")
    other = 1 - book
    rows, dim = vec_ref.shape
    width = dim // CHUNKS
    slots = n * cap
    f32, bf16, i32 = jnp.float32, jnp.bfloat16, jnp.int32

    barrier = pltpu.get_barrier_semaphore()

    def greet(step, carry):
        peer = lax.rem(me + step, n)
        pl.semaphore_signal(barrier, inc=1, device_id=(peer, book), device_id_type=MESH)
        pl.semaphore_signal(barrier, inc=1, device_id=(peer, other), device_id_type=MESH)
        return carry

    pl.semaphore_signal(barrier, inc=1, device_id=(me, other), device_id_type=MESH)
    lax.fori_loop(1, n, greet, 0)
    pl.semaphore_wait(barrier, 2 * n - 1)

    def code_copy(step):
        peer = lax.rem(me + step, n)
        return pltpu.make_async_remote_copy(
            src_ref=codes_ref,
            dst_ref=allc.at[me],
            send_sem=code_send.at[step],
            recv_sem=code_recv.at[me],
            device_id=(peer, book),
            device_id_type=MESH,
        )

    def start_codes(step, carry):
        code_copy(step).start()
        return carry

    lax.fori_loop(1, n, start_codes, 0)

    earlier = (
        lax.broadcasted_iota(i32, (rows, rows), 0) < lax.broadcasted_iota(i32, (rows, rows), 1)
    ).astype(bf16)
    mine = codes_ref[...]
    first, second = mine[0:1, :], mine[1:2, :]
    own_code = jnp.where(book == 0, first, second)
    oth_code = jnp.where(book == 0, second, first)

    def slot_table(code):
        target = code // own
        hits = (target == lax.broadcasted_iota(i32, (n, rows), 0)).astype(f32)
        before = jnp.dot(hits.astype(bf16), earlier, preferred_element_type=f32)
        rank = jnp.sum(before * hits, axis=0, keepdims=True)
        slot = target * cap + rank.astype(i32)
        return (slot == lax.broadcasted_iota(i32, (slots, rows), 0)).astype(f32)

    send_table = slot_table(own_code).astype(bf16)
    merge_table = jnp.transpose(slot_table(oth_code)).astype(bf16)

    allc[me] = mine

    def wait_codes(step, carry):
        source = lax.rem(me + step, n)
        whole(allc.at[source], code_recv.at[source]).wait()
        return carry

    lax.fori_loop(1, n, wait_codes, 0)

    all_codes = allc[...]
    firsts, seconds = all_codes[:, 0, :], all_codes[:, 1, :]
    own_all = jnp.where(book == 0, firsts, seconds)
    oth_all = jnp.where(book == 0, seconds, firsts)
    local = own_all - me * own
    inside = (local >= 0) & (local < own)
    before = jnp.dot(
        jnp.where(inside, 1.0, 0.0).astype(bf16), earlier, preferred_element_type=f32
    )
    rank = jnp.where(inside, before, -1.0).astype(i32)
    chosen = rank[:, None, :] == lax.broadcasted_iota(i32, (n, cap, rows), 1)
    local_one = (local + 1).astype(f32)
    oth_one = (oth_all + 1).astype(f32)
    row_code = jnp.sum(jnp.where(chosen, local_one[:, None, :], 0.0), axis=2, keepdims=True)
    oth_slot = jnp.sum(jnp.where(chosen, oth_one[:, None, :], 0.0), axis=2, keepdims=True)
    row_code = row_code.reshape(slots, 1).astype(i32) - 1
    oth_slot = oth_slot.reshape(slots, 1).astype(i32) - 1
    member32 = (row_code == lax.broadcasted_iota(i32, (slots, own), 1)).astype(f32)
    member = member32.astype(bf16)

    for c in range(CHUNKS):
        part = jnp.dot(
            member, book_ref[:, c * width : (c + 1) * width], preferred_element_type=f32
        )
        picks[c] = part.astype(bf16).reshape(n, cap, width)

        def start_one(step, carry):
            peer = lax.rem(me + step, n)
            pltpu.make_async_remote_copy(
                src_ref=picks.at[c, peer],
                dst_ref=ret.at[c, me],
                send_sem=one_send.at[c],
                recv_sem=one_recv.at[c],
                device_id=(peer, other),
                device_id_type=MESH,
            ).start()
            return carry

        lax.fori_loop(0, n, start_one, 0)

    memv[...] = jnp.transpose(member32).astype(bf16)
    group = 4

    def count_pairs(q, carry):
        columns = lax.broadcasted_iota(i32, (slots, group * BLK), 1) + q * (group * BLK)
        onehot = (oth_slot == columns).astype(f32).astype(bf16)
        counts = jnp.dot(memv[...], onehot, preferred_element_type=f32)
        for i in range(group):
            tabv[q * group + i] = counts[:, i * BLK : (i + 1) * BLK]
        return carry

    lax.fori_loop(0, KB // group, count_pairs, 0)
    table_copy = pltpu.make_async_copy(tabv, table_ref, out_sem.at[0])
    table_copy.start()
    member_copy = pltpu.make_async_copy(memv, member_ref, out_sem.at[1])
    member_copy.start()

    for c in range(CHUNKS):
        whole(ret.at[c], one_recv.at[c]).wait()
        rows_in = ret[c].reshape(slots, width)
        fetched = jnp.dot(merge_table, rows_in, preferred_element_type=f32)
        target = vec_ref[:, c * width : (c + 1) * width].astype(f32) - fetched
        part = jnp.dot(send_table, target.astype(bf16), preferred_element_type=f32)
        send[c] = part.astype(bf16).reshape(n, cap, width)

        def start_two(step, carry):
            peer = lax.rem(me + step, n)
            pltpu.make_async_remote_copy(
                src_ref=send.at[c, peer],
                dst_ref=got_ref.at[c, me],
                send_sem=two_send.at[c],
                recv_sem=two_recv.at[c],
                device_id=(peer, book),
                device_id_type=MESH,
            ).start()
            return carry

        lax.fori_loop(1, n, start_two, 0)
        pltpu.make_async_copy(send.at[c, me], got_ref.at[c, me], local_sem.at[c]).start()

    def wait_code_sends(step, carry):
        code_copy(step).wait_send()
        return carry

    lax.fori_loop(1, n, wait_code_sends, 0)
    table_copy.wait()
    member_copy.wait()
    for c in range(CHUNKS):
        whole(picks.at[c], one_send.at[c]).wait()
        whole(send.at[c, pl.ds(0, n - 1)], two_send.at[c]).wait()
        pltpu.make_async_copy(send.at[c, me], got_ref.at[c, me], local_sem.at[c]).wait()
        whole(got_ref.at[c, pl.ds(0, n - 1)], two_recv.at[c]).wait()


def finish_kernel(
    pieces, pairs_ref, got_ref, member_ref, table_ref, new_ref, gram_ref, tabv, newv, sems
):
    me = lax.axis_index("ingest")
    book = lax.axis_index("codes")
    first_row = book * KB + me * pieces
    other_start = (1 - book) * KB
    load = pltpu.make_async_copy(table_ref, tabv, sems.at[0])
    load.start()
    f32 = jnp.float32
    member = member_ref[...]
    load.wait()

    for piece in range(pieces):

        def place(p, carry):
            block = pairs_ref[first_row + piece, p] - other_start
            pltpu.make_async_copy(
                tabv.at[block, pl.ds(piece * BLK, BLK)],
                gram_ref.at[0, pl.ds(piece * BLK, BLK), pl.ds(pl.multiple_of(p * BLK, BLK), BLK)],
                sems.at[1],
            ).start()
            return carry

        lax.fori_loop(0, P_SIZE, place, 0)

    count = jnp.sum(member.astype(f32), axis=1, keepdims=True)
    scale = 1.0 / (count + 2.0)
    slots = member.shape[1]
    width = got_ref.shape[-1]
    for c in range(CHUNKS):
        rows_in = got_ref[c].reshape(slots, width)
        total = jnp.dot(member, rows_in, preferred_element_type=f32)
        newv[0, :, c * width : (c + 1) * width] = total * scale
    store = pltpu.make_async_copy(newv, new_ref, sems.at[0])
    store.start()
    store.wait()
    whole(gram_ref, sems.at[1]).wait()


def two_books(vectors, codes, codebook, pairs):
    n = lax.axis_size("ingest")
    rows, dim = vectors.shape
    own = codebook.shape[1]
    cap = 2 * rows // n
    slots = n * cap
    width = dim // CHUNKS
    f32, bf16 = jnp.float32, jnp.bfloat16
    vmem = pl.BlockSpec(memory_space=pltpu.VMEM)
    anywhere = pl.BlockSpec(memory_space=pl.ANY)
    dma = pltpu.SemaphoreType.DMA
    block = (CHUNKS, n, cap, width)
    got, table, member = pl.pallas_call(
        functools.partial(exchange_kernel, n, own, cap),
        out_shape=(
            jax.ShapeDtypeStruct(block, bf16),
            jax.ShapeDtypeStruct((KB, own, BLK), f32),
            jax.ShapeDtypeStruct((own, slots), bf16),
        ),
        in_specs=[vmem] * 3,
        out_specs=(anywhere,) * 3,
        scratch_shapes=[
            pltpu.VMEM((n,) + codes.shape, jnp.int32),
            pltpu.VMEM(block, bf16),
            pltpu.VMEM(block, bf16),
            pltpu.VMEM(block, bf16),
            pltpu.VMEM((KB, own, BLK), f32),
            pltpu.VMEM((own, slots), bf16),
            dma((n,)),
            dma((n,)),
            dma((CHUNKS,)),
            dma((CHUNKS,)),
            dma((CHUNKS,)),
            dma((CHUNKS,)),
            dma((CHUNKS,)),
            dma((2,)),
        ],
        compiler_params=pltpu.CompilerParams(
            collective_id=0, has_side_effects=True, vmem_limit_bytes=VMEM_BYTES
        ),
        name="exchange",
    )(codes, vectors, codebook[0])
    return pl.pallas_call(
        functools.partial(finish_kernel, own // BLK),
        out_shape=(
            jax.ShapeDtypeStruct((1, own, dim), f32),
            jax.ShapeDtypeStruct((1, own, P_SIZE * BLK), f32),
        ),
        in_specs=[pl.BlockSpec(memory_space=pltpu.SMEM), vmem, vmem, anywhere],
        out_specs=(anywhere, anywhere),
        scratch_shapes=[
            pltpu.VMEM((KB, own, BLK), f32),
            pltpu.VMEM((1, own, dim), f32),
            dma((2,)),
        ],
        compiler_params=pltpu.CompilerParams(vmem_limit_bytes=VMEM_BYTES),
        name="finish",
    )(pairs, got, member, table)


def shards(vectors, codes, codebook, pairs):
    owners = lax.axis_size("ingest")
    my_owner = lax.axis_index("ingest")
    my_group = lax.axis_index("codes")
    rows_count = vectors.shape[0]
    books_dev = codebook.shape[0]
    own_rows = codebook.shape[1]
    feature_dim = codebook.shape[2]
    codebooks = codes.shape[0]
    capacity = 2 * rows_count // owners
    slot_total = owners * books_dev * capacity
    local_codes = lax.dynamic_slice_in_dim(codes, my_group * books_dev, books_dev, 0)
    target = local_codes // own_rows
    within = local_codes - target * own_rows
    owner_hits = (target[:, :, None] == jnp.arange(owners, dtype=jnp.int32)).astype(jnp.int32)
    before = jnp.cumsum(owner_hits, axis=1) - owner_hits
    slot_rank = jnp.sum(before * owner_hits, axis=2)
    book_offset = jnp.arange(books_dev, dtype=jnp.int32)[:, None]
    slot_index = (target * books_dev + book_offset) * capacity + slot_rank
    slot_flat = slot_index.reshape(-1)
    vector_ids = jnp.broadcast_to(
        jnp.arange(rows_count, dtype=jnp.int32), (books_dev, rows_count)
    ).reshape(-1)
    slot_vector = jnp.full((slot_total,), rows_count, jnp.int32).at[slot_flat].set(vector_ids)
    asked_rows = (within + book_offset * own_rows).reshape(-1)
    slot_request = jnp.full((slot_total,), -1, jnp.int32).at[slot_flat].set(asked_rows)
    slot_request = slot_request.reshape(owners, books_dev * capacity)
    flat_book = codebook.reshape(books_dev * own_rows, feature_dim)
    picked = jnp.take(
        flat_book,
        jnp.maximum(
            lax.all_to_all(slot_request, "ingest", split_axis=0, concat_axis=0, tiled=True), 0
        ),
        axis=0,
    )
    returned = lax.all_to_all(picked, "ingest", split_axis=0, concat_axis=0, tiled=True)
    fetched = jnp.take(returned.reshape(slot_total, feature_dim), slot_index, axis=0)
    partial_sum = jnp.sum(fetched.astype(jnp.float32), axis=0)
    full_sum = lax.psum(partial_sum.astype(jnp.bfloat16), "codes").astype(jnp.float32)
    residual = (vectors.astype(jnp.float32) - full_sum).astype(jnp.bfloat16)
    residual_ext = jnp.concatenate([residual, jnp.zeros((1, feature_dim), jnp.bfloat16)], axis=0)
    codes_ext = jnp.concatenate([codes.T, jnp.full((1, codebooks), -1, jnp.int32)], axis=0)
    send_rows = jnp.take(residual_ext, slot_vector, axis=0).reshape(
        owners, books_dev * capacity, feature_dim
    )
    send_codes = jnp.take(codes_ext, slot_vector, axis=0).reshape(
        owners, books_dev * capacity, codebooks
    )
    got_rows, got_codes = (
        lax.all_to_all(send_rows, "ingest", split_axis=0, concat_axis=0, tiled=True),
        lax.all_to_all(send_codes, "ingest", split_axis=0, concat_axis=0, tiled=True),
    )
    got_rows = got_rows.reshape(owners, books_dev, capacity, feature_dim)
    got_codes = got_codes.reshape(owners, books_dev, capacity, codebooks)
    block_rows = min(own_rows, BLK)
    pieces = own_rows // block_rows
    group_size = min(P_SIZE, 8)
    contract = (((0,), (0,)), ((), ()))
    rows_in = got_rows[:, 0].reshape(owners * capacity, feature_dim)
    tuples = got_codes[:, 0].reshape(owners * capacity, codebooks)
    book_global = my_group * books_dev + 0
    own_code = lax.dynamic_index_in_dim(tuples, book_global, 1, keepdims=False)
    local_row = own_code - my_owner * own_rows
    member = (local_row[:, None] == jnp.arange(own_rows, dtype=jnp.int32)).astype(jnp.bfloat16)
    right_side = lax.dot_general(member, rows_in, contract, preferred_element_type=jnp.float32)
    code_count = jnp.sum(member, axis=0, dtype=jnp.float32)
    current = codebook[0].astype(jnp.float32)
    updated_list = [current + (right_side - 2.0 * current) / (code_count[:, None] + 2.0)]
    gram_pieces = []
    for part_index in range(pieces):
        first_row = book_global * K + my_owner * own_rows + part_index * block_rows
        partner = lax.dynamic_index_in_dim(pairs, first_row // BLK, 0, keepdims=False)
        partner_book = partner // KB
        partner_start = partner % KB * BLK
        partner_code = jnp.take(tuples, partner_book, axis=1) - partner_start[None, :]
        member_part = member[:, part_index * block_rows : (part_index + 1) * block_rows]
        columns = []
        for group_index in range(P_SIZE // group_size):
            chosen = partner_code[:, group_index * group_size : (group_index + 1) * group_size]
            onehot_table = (chosen[:, :, None] == jnp.arange(BLK, dtype=jnp.int32)).astype(
                jnp.bfloat16
            )
            onehot_table = onehot_table.reshape(chosen.shape[0], group_size * BLK)
            columns.append(
                lax.dot_general(
                    member_part, onehot_table, contract, preferred_element_type=jnp.float32
                )
            )
        gram_pieces.append(jnp.concatenate(columns, axis=1))
    gram_list = [jnp.concatenate(gram_pieces, axis=0)]
    return (jnp.stack(updated_list), jnp.stack(gram_list))


def solution(mesh):
    in_specs = (P("ingest", None), P(None, "ingest"), P("codes", "ingest", None), P())
    out_specs = (P("codes", "ingest", None), P("codes", "ingest", None))
    part = two_books if mesh.shape["codes"] == 2 else shards
    return jax.shard_map(part, mesh=mesh, in_specs=in_specs, out_specs=out_specs, check_vma=False)
```

```python
import functools

import jax
import jax.numpy as jnp
from jax import lax
from jax.experimental import pallas as pl
from jax.experimental.pallas import tpu as pltpu
from jax.sharding import PartitionSpec as P

K = 4096
BLK = 128
P_SIZE = 64
KB = 32
CHUNKS = 2
MESH = pl.DeviceIdType.MESH
VMEM_BYTES = 32 * 1024 * 1024


def whole(ref, sem):
    return pltpu.make_async_copy(ref, ref, sem)


def exchange_kernel(
    n, own, cap,
    codes_hbm, vec_hbm, book_hbm, pairs_hbm,
    got_ref, table_ref, member_ref, pairs_out,
    codes_ref, vec_ref, book_ref, allc, picks, ret, send,
    code_send, code_recv, one_send, one_recv, two_send, two_recv, local_sem, in_sem,
):
    me = lax.axis_index("ingest")
    book = lax.axis_index("codes")
    other = 1 - book
    rows, dim = vec_ref.shape
    width = dim // CHUNKS
    slots = n * cap
    f32, bf16, i32 = jnp.float32, jnp.bfloat16, jnp.int32

    load_codes = pltpu.make_async_copy(codes_hbm, codes_ref, in_sem.at[0])
    load_codes.start()
    load_book = pltpu.make_async_copy(book_hbm, book_ref, in_sem.at[1])
    load_book.start()
    load_vectors = pltpu.make_async_copy(vec_hbm, vec_ref, in_sem.at[2])
    load_vectors.start()
    load_pairs = pltpu.make_async_copy(pairs_hbm, pairs_out, in_sem.at[3])
    load_pairs.start()

    barrier = pltpu.get_barrier_semaphore()

    def greet(step, carry):
        peer = lax.rem(me + step, n)
        pl.semaphore_signal(barrier, inc=1, device_id=(peer, book), device_id_type=MESH)
        pl.semaphore_signal(barrier, inc=1, device_id=(peer, other), device_id_type=MESH)
        return carry

    pl.semaphore_signal(barrier, inc=1, device_id=(me, other), device_id_type=MESH)
    lax.fori_loop(1, n, greet, 0)
    load_codes.wait()
    pl.semaphore_wait(barrier, 2 * n - 1)

    def code_copy(step):
        peer = lax.rem(me + step, n)
        return pltpu.make_async_remote_copy(
            src_ref=codes_ref,
            dst_ref=allc.at[me],
            send_sem=code_send.at[step],
            recv_sem=code_recv.at[me],
            device_id=(peer, book),
            device_id_type=MESH,
        )

    def start_codes(step, carry):
        code_copy(step).start()
        return carry

    lax.fori_loop(1, n, start_codes, 0)

    earlier = (
        lax.broadcasted_iota(i32, (rows, rows), 0) < lax.broadcasted_iota(i32, (rows, rows), 1)
    ).astype(bf16)
    mine = codes_ref[...]
    first, second = mine[0:1, :], mine[1:2, :]
    own_code = jnp.where(book == 0, first, second)
    oth_code = jnp.where(book == 0, second, first)

    def slot_table(code):
        target = code // own
        hits = (target == lax.broadcasted_iota(i32, (n, rows), 0)).astype(f32)
        before = jnp.dot(hits.astype(bf16), earlier, preferred_element_type=f32)
        rank = jnp.sum(before * hits, axis=0, keepdims=True)
        slot = target * cap + rank.astype(i32)
        return (slot == lax.broadcasted_iota(i32, (slots, rows), 0)).astype(f32)

    send_table = slot_table(own_code).astype(bf16)
    merge_table = jnp.transpose(slot_table(oth_code)).astype(bf16)

    allc[me] = mine

    def wait_codes(step, carry):
        source = lax.rem(me + step, n)
        whole(allc.at[source], code_recv.at[source]).wait()
        return carry

    lax.fori_loop(1, n, wait_codes, 0)

    all_codes = allc[...]
    firsts, seconds = all_codes[:, 0, :], all_codes[:, 1, :]
    own_all = jnp.where(book == 0, firsts, seconds)
    oth_all = jnp.where(book == 0, seconds, firsts)
    local = own_all - me * own
    inside = (local >= 0) & (local < own)
    before = jnp.dot(
        jnp.where(inside, 1.0, 0.0).astype(bf16), earlier, preferred_element_type=f32
    )
    rank = jnp.where(inside, before, -1.0).astype(i32)
    chosen = rank[:, None, :] == lax.broadcasted_iota(i32, (n, cap, rows), 1)
    local_one = (local + 1).astype(f32)
    row_code = jnp.sum(jnp.where(chosen, local_one[:, None, :], 0.0), axis=2, keepdims=True)
    row_code = row_code.reshape(slots, 1).astype(i32) - 1
    member32 = (row_code == lax.broadcasted_iota(i32, (slots, own), 1)).astype(f32)
    member = member32.astype(bf16)

    load_book.wait()

    for c in range(CHUNKS):
        part = jnp.dot(
            member, book_ref[:, c * width : (c + 1) * width], preferred_element_type=f32
        )
        picks[c] = part.astype(bf16).reshape(n, cap, width)

        def start_one(step, carry):
            peer = lax.rem(me + step, n)
            pltpu.make_async_remote_copy(
                src_ref=picks.at[c, peer],
                dst_ref=ret.at[c, me],
                send_sem=one_send.at[c],
                recv_sem=one_recv.at[c],
                device_id=(peer, other),
                device_id_type=MESH,
            ).start()
            return carry

        lax.fori_loop(0, n, start_one, 0)

    oth_one = (oth_all + 1).astype(f32)
    oth_slot = jnp.sum(jnp.where(chosen, oth_one[:, None, :], 0.0), axis=2, keepdims=True)
    oth_slot = oth_slot.reshape(slots, 1).astype(i32) - 1
    member_ref[...] = jnp.transpose(member32).astype(bf16)
    group = 4

    def count_pairs(q, carry):
        columns = lax.broadcasted_iota(i32, (slots, group * BLK), 1) + q * (group * BLK)
        onehot = (oth_slot == columns).astype(f32).astype(bf16)
        counts = jnp.dot(member_ref[...], onehot, preferred_element_type=f32)
        for i in range(group):
            table_ref[q * group + i] = counts[:, i * BLK : (i + 1) * BLK]
        return carry

    lax.fori_loop(0, KB // group, count_pairs, 0)
    load_vectors.wait()
    load_pairs.wait()

    for c in range(CHUNKS):
        whole(ret.at[c], one_recv.at[c]).wait()
        rows_in = ret[c].reshape(slots, width)
        fetched = jnp.dot(merge_table, rows_in, preferred_element_type=f32)
        target = vec_ref[:, c * width : (c + 1) * width].astype(f32) - fetched
        part = jnp.dot(send_table, target.astype(bf16), preferred_element_type=f32)
        send[c] = part.astype(bf16).reshape(n, cap, width)

        def start_two(step, carry):
            peer = lax.rem(me + step, n)
            pltpu.make_async_remote_copy(
                src_ref=send.at[c, peer],
                dst_ref=got_ref.at[c, me],
                send_sem=two_send.at[c],
                recv_sem=two_recv.at[c],
                device_id=(peer, book),
                device_id_type=MESH,
            ).start()
            return carry

        lax.fori_loop(1, n, start_two, 0)
        pltpu.make_async_copy(send.at[c, me], got_ref.at[c, me], local_sem.at[c]).start()

    def wait_code_sends(step, carry):
        code_copy(step).wait_send()
        return carry

    lax.fori_loop(1, n, wait_code_sends, 0)
    for c in range(CHUNKS):
        whole(picks.at[c], one_send.at[c]).wait()
        whole(send.at[c, pl.ds(0, n - 1)], two_send.at[c]).wait()
        pltpu.make_async_copy(send.at[c, me], got_ref.at[c, me], local_sem.at[c]).wait()
        whole(got_ref.at[c, pl.ds(0, n - 1)], two_recv.at[c]).wait()


def finish_kernel(
    pieces, pairs_in, got_ref, member_ref, table_ref, new_ref, gram_ref, pairs_ref, newv, sems
):
    me = lax.axis_index("ingest")
    book = lax.axis_index("codes")
    first_row = book * KB + me * pieces
    other_start = (1 - book) * KB
    load = pltpu.make_async_copy(pairs_in, pairs_ref, sems.at[0])
    load.start()
    f32 = jnp.float32
    member = member_ref[...]
    load.wait()

    for piece in range(pieces):

        def place(p, carry):
            block = pairs_ref[first_row + piece, p] - other_start
            pltpu.make_async_copy(
                table_ref.at[block, pl.ds(piece * BLK, BLK)],
                gram_ref.at[0, pl.ds(piece * BLK, BLK), pl.ds(pl.multiple_of(p * BLK, BLK), BLK)],
                sems.at[1],
            ).start()
            return carry

        lax.fori_loop(0, P_SIZE, place, 0)

    count = jnp.sum(member.astype(f32), axis=1, keepdims=True)
    scale = 1.0 / (count + 2.0)
    slots = member.shape[1]
    width = got_ref.shape[-1]
    for c in range(CHUNKS):
        rows_in = got_ref[c].reshape(slots, width)
        total = jnp.dot(member, rows_in, preferred_element_type=f32)
        newv[0, :, c * width : (c + 1) * width] = total * scale
    store = pltpu.make_async_copy(newv, new_ref, sems.at[0])
    store.start()
    store.wait()
    whole(gram_ref, sems.at[1]).wait()


def two_books(vectors, codes, codebook, pairs):
    n = lax.axis_size("ingest")
    rows, dim = vectors.shape
    own = codebook.shape[1]
    cap = 2 * rows // n
    slots = n * cap
    width = dim // CHUNKS
    f32, bf16 = jnp.float32, jnp.bfloat16
    vmem = pl.BlockSpec(memory_space=pltpu.VMEM)
    hbm = pl.BlockSpec(memory_space=pltpu.HBM)
    dma = pltpu.SemaphoreType.DMA
    block = (CHUNKS, n, cap, width)
    got, table, member, pairs = pl.pallas_call(
        functools.partial(exchange_kernel, n, own, cap),
        out_shape=(
            jax.ShapeDtypeStruct(block, bf16),
            jax.ShapeDtypeStruct((KB, own, BLK), f32),
            jax.ShapeDtypeStruct((own, slots), bf16),
            jax.ShapeDtypeStruct(pairs.shape, jnp.int32),
        ),
        in_specs=[hbm] * 4,
        out_specs=(vmem,) * 4,
        scratch_shapes=[
            pltpu.VMEM(codes.shape, jnp.int32),
            pltpu.VMEM((rows, dim), bf16),
            pltpu.VMEM((own, dim), bf16),
            pltpu.VMEM((n,) + codes.shape, jnp.int32),
            pltpu.VMEM(block, bf16),
            pltpu.VMEM(block, bf16),
            pltpu.VMEM(block, bf16),
            dma((n,)),
            dma((n,)),
            dma((CHUNKS,)),
            dma((CHUNKS,)),
            dma((CHUNKS,)),
            dma((CHUNKS,)),
            dma((CHUNKS,)),
            dma((4,)),
        ],
        compiler_params=pltpu.CompilerParams(
            collective_id=0, has_side_effects=True, vmem_limit_bytes=VMEM_BYTES
        ),
        name="exchange",
    )(*(pltpu.with_memory_space_constraint(a, pltpu.HBM) for a in (codes, vectors, codebook[0], pairs)))
    return pl.pallas_call(
        functools.partial(finish_kernel, own // BLK),
        out_shape=(
            jax.ShapeDtypeStruct((1, own, dim), f32),
            jax.ShapeDtypeStruct((1, own, P_SIZE * BLK), f32),
        ),
        in_specs=[vmem] * 4,
        out_specs=(hbm, hbm),
        scratch_shapes=[
            pltpu.SMEM(pairs.shape, jnp.int32),
            pltpu.VMEM((1, own, dim), f32),
            dma((2,)),
        ],
        compiler_params=pltpu.CompilerParams(vmem_limit_bytes=16 * 1024 * 1024),
        name="finish",
    )(pairs, got, member, table)


def shards(vectors, codes, codebook, pairs):
    owners = lax.axis_size("ingest")
    my_owner = lax.axis_index("ingest")
    my_group = lax.axis_index("codes")
    rows_count = vectors.shape[0]
    books_dev = codebook.shape[0]
    own_rows = codebook.shape[1]
    feature_dim = codebook.shape[2]
    codebooks = codes.shape[0]
    capacity = 2 * rows_count // owners
    slot_total = owners * books_dev * capacity
    local_codes = lax.dynamic_slice_in_dim(codes, my_group * books_dev, books_dev, 0)
    target = local_codes // own_rows
    within = local_codes - target * own_rows
    owner_hits = (target[:, :, None] == jnp.arange(owners, dtype=jnp.int32)).astype(jnp.int32)
    before = jnp.cumsum(owner_hits, axis=1) - owner_hits
    slot_rank = jnp.sum(before * owner_hits, axis=2)
    book_offset = jnp.arange(books_dev, dtype=jnp.int32)[:, None]
    slot_index = (target * books_dev + book_offset) * capacity + slot_rank
    slot_flat = slot_index.reshape(-1)
    vector_ids = jnp.broadcast_to(
        jnp.arange(rows_count, dtype=jnp.int32), (books_dev, rows_count)
    ).reshape(-1)
    slot_vector = jnp.full((slot_total,), rows_count, jnp.int32).at[slot_flat].set(vector_ids)
    asked_rows = (within + book_offset * own_rows).reshape(-1)
    slot_request = jnp.full((slot_total,), -1, jnp.int32).at[slot_flat].set(asked_rows)
    slot_request = slot_request.reshape(owners, books_dev * capacity)
    flat_book = codebook.reshape(books_dev * own_rows, feature_dim)
    picked = jnp.take(
        flat_book,
        jnp.maximum(
            lax.all_to_all(slot_request, "ingest", split_axis=0, concat_axis=0, tiled=True), 0
        ),
        axis=0,
    )
    returned = lax.all_to_all(picked, "ingest", split_axis=0, concat_axis=0, tiled=True)
    fetched = jnp.take(returned.reshape(slot_total, feature_dim), slot_index, axis=0)
    partial_sum = jnp.sum(fetched.astype(jnp.float32), axis=0)
    full_sum = lax.psum(partial_sum.astype(jnp.bfloat16), "codes").astype(jnp.float32)
    residual = (vectors.astype(jnp.float32) - full_sum).astype(jnp.bfloat16)
    residual_ext = jnp.concatenate([residual, jnp.zeros((1, feature_dim), jnp.bfloat16)], axis=0)
    codes_ext = jnp.concatenate([codes.T, jnp.full((1, codebooks), -1, jnp.int32)], axis=0)
    send_rows = jnp.take(residual_ext, slot_vector, axis=0).reshape(
        owners, books_dev * capacity, feature_dim
    )
    send_codes = jnp.take(codes_ext, slot_vector, axis=0).reshape(
        owners, books_dev * capacity, codebooks
    )
    got_rows, got_codes = (
        lax.all_to_all(send_rows, "ingest", split_axis=0, concat_axis=0, tiled=True),
        lax.all_to_all(send_codes, "ingest", split_axis=0, concat_axis=0, tiled=True),
    )
    got_rows = got_rows.reshape(owners, books_dev, capacity, feature_dim)
    got_codes = got_codes.reshape(owners, books_dev, capacity, codebooks)
    block_rows = min(own_rows, BLK)
    pieces = own_rows // block_rows
    group_size = min(P_SIZE, 8)
    contract = (((0,), (0,)), ((), ()))
    rows_in = got_rows[:, 0].reshape(owners * capacity, feature_dim)
    tuples = got_codes[:, 0].reshape(owners * capacity, codebooks)
    book_global = my_group * books_dev + 0
    own_code = lax.dynamic_index_in_dim(tuples, book_global, 1, keepdims=False)
    local_row = own_code - my_owner * own_rows
    member = (local_row[:, None] == jnp.arange(own_rows, dtype=jnp.int32)).astype(jnp.bfloat16)
    right_side = lax.dot_general(member, rows_in, contract, preferred_element_type=jnp.float32)
    code_count = jnp.sum(member, axis=0, dtype=jnp.float32)
    current = codebook[0].astype(jnp.float32)
    updated_list = [current + (right_side - 2.0 * current) / (code_count[:, None] + 2.0)]
    gram_pieces = []
    for part_index in range(pieces):
        first_row = book_global * K + my_owner * own_rows + part_index * block_rows
        partner = lax.dynamic_index_in_dim(pairs, first_row // BLK, 0, keepdims=False)
        partner_book = partner // KB
        partner_start = partner % KB * BLK
        partner_code = jnp.take(tuples, partner_book, axis=1) - partner_start[None, :]
        member_part = member[:, part_index * block_rows : (part_index + 1) * block_rows]
        columns = []
        for group_index in range(P_SIZE // group_size):
            chosen = partner_code[:, group_index * group_size : (group_index + 1) * group_size]
            onehot_table = (chosen[:, :, None] == jnp.arange(BLK, dtype=jnp.int32)).astype(
                jnp.bfloat16
            )
            onehot_table = onehot_table.reshape(chosen.shape[0], group_size * BLK)
            columns.append(
                lax.dot_general(
                    member_part, onehot_table, contract, preferred_element_type=jnp.float32
                )
            )
        gram_pieces.append(jnp.concatenate(columns, axis=1))
    gram_list = [jnp.concatenate(gram_pieces, axis=0)]
    return (jnp.stack(updated_list), jnp.stack(gram_list))


def solution(mesh):
    in_specs = (P("ingest", None), P(None, "ingest"), P("codes", "ingest", None), P())
    out_specs = (P("codes", "ingest", None), P("codes", "ingest", None))
    part = two_books if mesh.shape["codes"] == 2 else shards
    return jax.shard_map(part, mesh=mesh, in_specs=in_specs, out_specs=out_specs, check_vma=False)
```

```python
import functools

import jax
import jax.numpy as jnp
from jax import lax
from jax.experimental import pallas as pl
from jax.experimental.pallas import tpu as pltpu
from jax.sharding import PartitionSpec as P

K = 4096
BLK = 128
P_SIZE = 64
KB = 32
CHUNKS = 4
PLANE = 4
MESH = pl.DeviceIdType.MESH
VMEM_BYTES = 32 * 1024 * 1024


def whole(ref, sem):
    return pltpu.make_async_copy(ref, ref, sem)


def exchange_kernel(
    n, own, cap,
    codes_hbm, vec_hbm, book_hbm, pairs_hbm,
    got_ref, table_ref, member_ref, book_ref, pairs_out,
    codes_ref, vec_ref, allc, picks, ret, send, table, merge, acc,
    up_out, up_in, down_out, down_in, cast,
    code_send, code_recv, one_send, one_recv, two_send, two_recv, local_sem,
    up_send, up_recv, down_send, down_recv, cast_up, cast_down, cast_recv, in_sem,
):
    me = lax.axis_index("ingest")
    book = lax.axis_index("codes")
    other = 1 - book
    rows, dim = vec_ref.shape
    half = dim // 2
    width = half // CHUNKS
    slots = n * cap
    planes = n // PLANE
    plane = me // PLANE
    place = me % PLANE
    peers = 2 * PLANE
    my_peer = book * PLANE + place
    above = me + PLANE
    below = me - PLANE
    f32, bf16, i32 = jnp.float32, jnp.bfloat16, jnp.int32

    load_codes = pltpu.make_async_copy(codes_hbm, codes_ref, in_sem.at[0])
    load_codes.start()
    load_book = pltpu.make_async_copy(book_hbm, book_ref, in_sem.at[1])
    load_book.start()
    load_vectors = pltpu.make_async_copy(vec_hbm, vec_ref, in_sem.at[2])
    load_vectors.start()
    load_pairs = pltpu.make_async_copy(pairs_hbm, pairs_out, in_sem.at[3])
    load_pairs.start()

    barrier = pltpu.get_barrier_semaphore()

    def greet(step, carry):
        peer = lax.rem(me + step, n)
        pl.semaphore_signal(barrier, inc=1, device_id=(peer, book), device_id_type=MESH)
        return carry

    def greet_plane(step, carry):
        peer = plane * PLANE + step
        pl.semaphore_signal(barrier, inc=1, device_id=(peer, other), device_id_type=MESH)
        return carry

    lax.fori_loop(1, n, greet, 0)
    lax.fori_loop(0, PLANE, greet_plane, 0)
    load_codes.wait()
    pl.semaphore_wait(barrier, n - 1 + PLANE)

    def code_copy(step):
        peer = lax.rem(me + step, n)
        return pltpu.make_async_remote_copy(
            src_ref=codes_ref,
            dst_ref=allc.at[place * planes + plane],
            send_sem=code_send.at[step],
            recv_sem=code_recv.at[place * planes + plane],
            device_id=(peer, book),
            device_id_type=MESH,
        )

    def start_codes(step, carry):
        code_copy(step).start()
        return carry

    lax.fori_loop(1, n, start_codes, 0)
    earlier = (
        lax.broadcasted_iota(i32, (rows, rows), 0) < lax.broadcasted_iota(i32, (rows, rows), 1)
    ).astype(bf16)
    allc[place * planes + plane] = codes_ref[...]

    def wait_codes(step, carry):
        peer = lax.rem(me + step, n)
        source = peer % PLANE * planes + peer // PLANE
        whole(allc.at[source], code_recv.at[source]).wait()
        return carry

    lax.fori_loop(1, n, wait_codes, 0)

    all_codes = allc[...]
    firsts, seconds = all_codes[:, 0, :], all_codes[:, 1, :]
    own_all = jnp.where(book == 0, firsts, seconds)
    oth_all = jnp.where(book == 0, seconds, firsts)
    local = own_all - me * own
    inside = (local >= 0) & (local < own)
    before = jnp.dot(
        jnp.where(inside, 1.0, 0.0).astype(bf16), earlier, preferred_element_type=f32
    )
    rank = jnp.where(inside, before, -1.0).astype(i32)
    chosen = rank[:, None, :] == lax.broadcasted_iota(i32, (n, cap, rows), 1)
    local_one = (local + 1).astype(f32)
    row_code = jnp.sum(jnp.where(chosen, local_one[:, None, :], 0.0), axis=2, keepdims=True)
    row_code = row_code.reshape(slots, 1).astype(i32) - 1
    member32 = (row_code == lax.broadcasted_iota(i32, (slots, own), 1)).astype(f32)
    member = member32.astype(bf16)
    load_book.wait()

    def plane_copy(step, c, source, target, send_sem, recv_sem):
        q = lax.rem(my_peer + step, peers)
        return pltpu.make_async_remote_copy(
            src_ref=source.at[c, q],
            dst_ref=target.at[c, my_peer],
            send_sem=send_sem.at[c],
            recv_sem=recv_sem.at[c],
            device_id=(plane * PLANE + q % PLANE, q // PLANE),
            device_id_type=MESH,
        )

    def plane_start(c, source, target, send_sem, recv_sem, own_sem):
        def start(step, carry):
            plane_copy(step, c, source, target, send_sem, recv_sem).start()
            return carry

        lax.fori_loop(1, peers, start, 0)
        pltpu.make_async_copy(source.at[c, my_peer], target.at[c, my_peer], own_sem).start()

    def plane_wait(c, source, target, recv_sem, own_sem):
        pltpu.make_async_copy(source.at[c, my_peer], target.at[c, my_peer], own_sem).wait()
        whole(target.at[c, pl.ds(0, peers - 1)], recv_sem.at[c]).wait()

    for c in range(CHUNKS):
        for core in range(2):
            at = core * half + c * width
            part = jnp.dot(member, book_ref[:, at : at + width], preferred_element_type=f32)
            picks[c, core * PLANE : (core + 1) * PLANE] = part.astype(bf16).reshape(
                PLANE, planes, cap, width
            )
        plane_start(c, picks, ret, one_send, one_recv, local_sem.at[0, c])

    column = allc[pl.ds(place * planes, planes)]
    for d in range(planes):
        parts = []
        for m in range(2):
            code = column[d, m : m + 1, :]
            target = code // own
            hits = (target == lax.broadcasted_iota(i32, (n, rows), 0)).astype(f32)
            ahead = jnp.dot(hits.astype(bf16), earlier, preferred_element_type=f32)
            rank_row = jnp.sum(ahead * hits, axis=0, keepdims=True).astype(i32)
            slot = (target - plane * PLANE) * cap + rank_row
            inner = lax.broadcasted_iota(i32, (PLANE * cap, rows), 0)
            parts.append((slot == inner).astype(f32))
        both = jnp.concatenate(parts, axis=0)
        table[d] = both.astype(bf16)
        merge[d] = jnp.transpose(both).astype(bf16)

    oth_one = (oth_all + 1).astype(f32)
    oth_slot = jnp.sum(jnp.where(chosen, oth_one[:, None, :], 0.0), axis=2, keepdims=True)
    oth_slot = oth_slot.reshape(slots, 1).astype(i32) - 1
    member_ref[...] = jnp.transpose(member32).astype(bf16)
    group = 4

    def count_pairs(q, carry):
        columns = lax.broadcasted_iota(i32, (slots, group * BLK), 1) + q * (group * BLK)
        onehot = (oth_slot == columns).astype(f32).astype(bf16)
        counts = jnp.dot(member_ref[...], onehot, preferred_element_type=f32)
        for i in range(group):
            table_ref[q * group + i] = counts[:, i * BLK : (i + 1) * BLK]
        return carry

    def partial_sum(c, d):
        rows_in = ret[c, :, d].reshape(peers * cap, width)
        return jnp.dot(merge[d], rows_in, preferred_element_type=f32)

    def up_copy(c, d):
        return pltpu.make_async_remote_copy(
            src_ref=up_out.at[c, d], dst_ref=up_in.at[c, d],
            send_sem=up_send.at[c, d], recv_sem=up_recv.at[c, d],
            device_id=(above, book), device_id_type=MESH,
        )

    def down_copy(c, d):
        return pltpu.make_async_remote_copy(
            src_ref=down_out.at[c, d], dst_ref=down_in.at[c, d],
            send_sem=down_send.at[c, d], recv_sem=down_recv.at[c, d],
            device_id=(below, book), device_id_type=MESH,
        )

    def cast_copy(c, d, upward):
        return pltpu.make_async_remote_copy(
            src_ref=cast.at[c, d], dst_ref=cast.at[c, d],
            send_sem=(cast_up if upward else cast_down).at[c, d], recv_sem=cast_recv.at[c, d],
            device_id=(above if upward else below, book), device_id_type=MESH,
        )

    def reduce_step(c):
        plane_wait(c, picks, ret, one_recv, local_sem.at[0, c])
        for k in range(planes - 1):
            d_up, d_down = planes - 1 - k, k

            @pl.when(plane < d_up)
            def _():
                acc[...] = partial_sum(c, d_up)

                @pl.when(plane > 0)
                def _():
                    whole(up_in.at[c, d_up], up_recv.at[c, d_up]).wait()
                    acc[...] += up_in[c, d_up].astype(f32)

                up_out[c, d_up] = acc[...].astype(bf16)
                up_copy(c, d_up).start()

            @pl.when(plane > d_down)
            def _():
                acc[...] = partial_sum(c, d_down)

                @pl.when(plane < planes - 1)
                def _():
                    whole(down_in.at[c, d_down], down_recv.at[c, d_down]).wait()
                    acc[...] += down_in[c, d_down].astype(f32)

                down_out[c, d_down] = acc[...].astype(bf16)
                down_copy(c, d_down).start()

    def residual_step(c):
        acc[...] = partial_sum(c, plane)

        @pl.when(plane > 0)
        def _():
            whole(up_in.at[c, plane], up_recv.at[c, plane]).wait()
            acc[...] += up_in[c, plane].astype(f32)

        @pl.when(plane < planes - 1)
        def _():
            whole(down_in.at[c, plane], down_recv.at[c, plane]).wait()
            acc[...] += down_in[c, plane].astype(f32)

        low = vec_ref[:, c * width : (c + 1) * width].astype(f32)
        high = vec_ref[:, half + c * width : half + (c + 1) * width].astype(f32)
        cast[c, plane] = (jnp.where(book == 0, low, high) - acc[...]).astype(bf16)

        @pl.when(plane < planes - 1)
        def _():
            cast_copy(c, plane, True).start()

        @pl.when(plane > 0)
        def _():
            cast_copy(c, plane, False).start()

    def spread_step(c):
        for k in range(1, planes):

            @pl.when(plane >= k)
            def _():
                whole(cast.at[c, plane - k], cast_recv.at[c, plane - k]).wait()

                @pl.when(plane < planes - 1)
                def _():
                    cast_copy(c, plane - k, True).start()

            @pl.when(plane + k < planes)
            def _():
                whole(cast.at[c, plane + k], cast_recv.at[c, plane + k]).wait()

                @pl.when(plane > 0)
                def _():
                    cast_copy(c, plane + k, False).start()

        for d in range(planes):
            part = jnp.dot(table[d], cast[c, d], preferred_element_type=f32)
            send[c, :, d] = part.astype(bf16).reshape(peers, cap, width)
        plane_start(c, send, got_ref, two_send, two_recv, local_sem.at[1, c])

    load_vectors.wait()
    load_pairs.wait()
    per_chunk = KB // group // CHUNKS
    for t in range(CHUNKS + 2):
        if t < CHUNKS:
            reduce_step(t)
            lax.fori_loop(t * per_chunk, (t + 1) * per_chunk, count_pairs, 0)
        if 1 <= t <= CHUNKS:
            residual_step(t - 1)
        if t >= 2:
            spread_step(t - 2)

    def wait_code_sends(step, carry):
        code_copy(step).wait_send()
        return carry

    lax.fori_loop(1, n, wait_code_sends, 0)
    for c in range(CHUNKS):
        whole(picks.at[c, pl.ds(0, peers - 1)], one_send.at[c]).wait()
        whole(send.at[c, pl.ds(0, peers - 1)], two_send.at[c]).wait()
        for d in range(planes):

            @pl.when(plane < d)
            def _():
                up_copy(c, d).wait_send()

            @pl.when(plane > d)
            def _():
                down_copy(c, d).wait_send()

            @pl.when((plane >= d) & (plane < planes - 1))
            def _():
                cast_copy(c, d, True).wait_send()

            @pl.when((plane <= d) & (plane > 0))
            def _():
                cast_copy(c, d, False).wait_send()

        plane_wait(c, send, got_ref, two_recv, local_sem.at[1, c])


def finish_kernel(
    pieces, pairs_in, got_ref, member_ref, table_ref, book_ref, new_ref, gram_ref, pairs_ref, newv, sems
):
    me = lax.axis_index("ingest")
    book = lax.axis_index("codes")
    first_row = book * KB + me * pieces
    other_start = (1 - book) * KB
    load = pltpu.make_async_copy(pairs_in, pairs_ref, sems.at[0])
    load.start()
    f32 = jnp.float32
    member = member_ref[...]
    load.wait()

    for piece in range(pieces):

        def place(p, carry):
            block = pairs_ref[first_row + piece, p] - other_start
            pltpu.make_async_copy(
                table_ref.at[block, pl.ds(piece * BLK, BLK)],
                gram_ref.at[0, pl.ds(piece * BLK, BLK), pl.ds(pl.multiple_of(p * BLK, BLK), BLK)],
                sems.at[1],
            ).start()
            return carry

        lax.fori_loop(0, P_SIZE, place, 0)

    count = jnp.sum(member.astype(f32), axis=1, keepdims=True)
    scale = 1.0 / (count + 2.0)
    slots = member.shape[1]
    width = got_ref.shape[-1]
    half = CHUNKS * width
    for c in range(CHUNKS):
        for core in range(2):
            rows_in = got_ref[c, core * PLANE : (core + 1) * PLANE].reshape(slots, width)
            total = jnp.dot(member, rows_in, preferred_element_type=f32)
            at = core * half + c * width
            current = book_ref[:, at : at + width].astype(f32)
            newv[0, :, at : at + width] = current + (total - 2.0 * current) * scale
    store = pltpu.make_async_copy(newv, new_ref, sems.at[0])
    store.start()
    store.wait()
    whole(gram_ref, sems.at[1]).wait()


def two_books(vectors, codes, codebook, pairs):
    n = lax.axis_size("ingest")
    rows, dim = vectors.shape
    own = codebook.shape[1]
    cap = 2 * rows // n
    slots = n * cap
    planes = n // PLANE
    width = dim // 2 // CHUNKS
    f32, bf16, i32 = jnp.float32, jnp.bfloat16, jnp.int32
    vmem = pl.BlockSpec(memory_space=pltpu.VMEM)
    hbm = pl.BlockSpec(memory_space=pltpu.HBM)
    dma = pltpu.SemaphoreType.DMA
    block = (CHUNKS, 2 * PLANE, planes, cap, width)
    dense = (CHUNKS, planes, rows, width)
    per_plane = dma((CHUNKS, planes))
    per_chunk = dma((CHUNKS,))
    held = [
        pltpu.with_memory_space_constraint(x, pltpu.HBM)
        for x in (codes, vectors, codebook[0], pairs)
    ]
    got, table, member, book, pairs = pl.pallas_call(
        functools.partial(exchange_kernel, n, own, cap),
        out_shape=(
            jax.ShapeDtypeStruct(block, bf16),
            jax.ShapeDtypeStruct((KB, own, BLK), f32),
            jax.ShapeDtypeStruct((own, slots), bf16),
            jax.ShapeDtypeStruct((own, dim), bf16),
            jax.ShapeDtypeStruct(pairs.shape, i32),
        ),
        in_specs=[hbm] * 4,
        out_specs=(vmem,) * 5,
        scratch_shapes=[
            pltpu.VMEM(codes.shape, i32),
            pltpu.VMEM((rows, dim), bf16),
            pltpu.VMEM((n,) + codes.shape, i32),
            pltpu.VMEM(block, bf16),
            pltpu.VMEM(block, bf16),
            pltpu.VMEM(block, bf16),
            pltpu.VMEM((planes, 2 * PLANE * cap, rows), bf16),
            pltpu.VMEM((planes, rows, 2 * PLANE * cap), bf16),
            pltpu.VMEM((rows, width), f32),
            pltpu.VMEM(dense, bf16),
            pltpu.VMEM(dense, bf16),
            pltpu.VMEM(dense, bf16),
            pltpu.VMEM(dense, bf16),
            pltpu.VMEM(dense, bf16),
            dma((n,)),
            dma((n,)),
            per_chunk,
            per_chunk,
            per_chunk,
            per_chunk,
            dma((2, CHUNKS)),
            per_plane,
            per_plane,
            per_plane,
            per_plane,
            per_plane,
            per_plane,
            per_plane,
            dma((4,)),
        ],
        compiler_params=pltpu.CompilerParams(
            collective_id=0, has_side_effects=True, vmem_limit_bytes=VMEM_BYTES
        ),
        name="exchange",
    )(*held)
    return pl.pallas_call(
        functools.partial(finish_kernel, own // BLK),
        out_shape=(
            jax.ShapeDtypeStruct((1, own, dim), f32),
            jax.ShapeDtypeStruct((1, own, P_SIZE * BLK), f32),
        ),
        in_specs=[vmem] * 5,
        out_specs=(hbm, hbm),
        scratch_shapes=[
            pltpu.SMEM(pairs.shape, i32),
            pltpu.VMEM((1, own, dim), f32),
            dma((2,)),
        ],
        compiler_params=pltpu.CompilerParams(vmem_limit_bytes=16 * 1024 * 1024),
        name="finish",
    )(pairs, got, member, table, book)


def shards(vectors, codes, codebook, pairs):
    owners = lax.axis_size("ingest")
    my_owner = lax.axis_index("ingest")
    my_group = lax.axis_index("codes")
    rows_count = vectors.shape[0]
    books_dev = codebook.shape[0]
    own_rows = codebook.shape[1]
    feature_dim = codebook.shape[2]
    codebooks = codes.shape[0]
    capacity = 2 * rows_count // owners
    slot_total = owners * books_dev * capacity
    local_codes = lax.dynamic_slice_in_dim(codes, my_group * books_dev, books_dev, 0)
    target = local_codes // own_rows
    within = local_codes - target * own_rows
    owner_hits = (target[:, :, None] == jnp.arange(owners, dtype=jnp.int32)).astype(jnp.int32)
    before = jnp.cumsum(owner_hits, axis=1) - owner_hits
    slot_rank = jnp.sum(before * owner_hits, axis=2)
    book_offset = jnp.arange(books_dev, dtype=jnp.int32)[:, None]
    slot_index = (target * books_dev + book_offset) * capacity + slot_rank
    slot_flat = slot_index.reshape(-1)
    vector_ids = jnp.broadcast_to(
        jnp.arange(rows_count, dtype=jnp.int32), (books_dev, rows_count)
    ).reshape(-1)
    slot_vector = jnp.full((slot_total,), rows_count, jnp.int32).at[slot_flat].set(vector_ids)
    asked_rows = (within + book_offset * own_rows).reshape(-1)
    slot_request = jnp.full((slot_total,), -1, jnp.int32).at[slot_flat].set(asked_rows)
    slot_request = slot_request.reshape(owners, books_dev * capacity)
    flat_book = codebook.reshape(books_dev * own_rows, feature_dim)
    picked = jnp.take(
        flat_book,
        jnp.maximum(
            lax.all_to_all(slot_request, "ingest", split_axis=0, concat_axis=0, tiled=True), 0
        ),
        axis=0,
    )
    returned = lax.all_to_all(picked, "ingest", split_axis=0, concat_axis=0, tiled=True)
    fetched = jnp.take(returned.reshape(slot_total, feature_dim), slot_index, axis=0)
    partial_sum = jnp.sum(fetched.astype(jnp.float32), axis=0)
    full_sum = lax.psum(partial_sum.astype(jnp.bfloat16), "codes").astype(jnp.float32)
    residual = (vectors.astype(jnp.float32) - full_sum).astype(jnp.bfloat16)
    residual_ext = jnp.concatenate([residual, jnp.zeros((1, feature_dim), jnp.bfloat16)], axis=0)
    codes_ext = jnp.concatenate([codes.T, jnp.full((1, codebooks), -1, jnp.int32)], axis=0)
    send_rows = jnp.take(residual_ext, slot_vector, axis=0).reshape(
        owners, books_dev * capacity, feature_dim
    )
    send_codes = jnp.take(codes_ext, slot_vector, axis=0).reshape(
        owners, books_dev * capacity, codebooks
    )
    got_rows, got_codes = (
        lax.all_to_all(send_rows, "ingest", split_axis=0, concat_axis=0, tiled=True),
        lax.all_to_all(send_codes, "ingest", split_axis=0, concat_axis=0, tiled=True),
    )
    got_rows = got_rows.reshape(owners, books_dev, capacity, feature_dim)
    got_codes = got_codes.reshape(owners, books_dev, capacity, codebooks)
    block_rows = min(own_rows, BLK)
    pieces = own_rows // block_rows
    group_size = min(P_SIZE, 8)
    contract = (((0,), (0,)), ((), ()))
    rows_in = got_rows[:, 0].reshape(owners * capacity, feature_dim)
    tuples = got_codes[:, 0].reshape(owners * capacity, codebooks)
    book_global = my_group * books_dev + 0
    own_code = lax.dynamic_index_in_dim(tuples, book_global, 1, keepdims=False)
    local_row = own_code - my_owner * own_rows
    member = (local_row[:, None] == jnp.arange(own_rows, dtype=jnp.int32)).astype(jnp.bfloat16)
    right_side = lax.dot_general(member, rows_in, contract, preferred_element_type=jnp.float32)
    code_count = jnp.sum(member, axis=0, dtype=jnp.float32)
    current = codebook[0].astype(jnp.float32)
    updated_list = [current + (right_side - 2.0 * current) / (code_count[:, None] + 2.0)]
    gram_pieces = []
    for part_index in range(pieces):
        first_row = book_global * K + my_owner * own_rows + part_index * block_rows
        partner = lax.dynamic_index_in_dim(pairs, first_row // BLK, 0, keepdims=False)
        partner_book = partner // KB
        partner_start = partner % KB * BLK
        partner_code = jnp.take(tuples, partner_book, axis=1) - partner_start[None, :]
        member_part = member[:, part_index * block_rows : (part_index + 1) * block_rows]
        columns = []
        for group_index in range(P_SIZE // group_size):
            chosen = partner_code[:, group_index * group_size : (group_index + 1) * group_size]
            onehot_table = (chosen[:, :, None] == jnp.arange(BLK, dtype=jnp.int32)).astype(
                jnp.bfloat16
            )
            onehot_table = onehot_table.reshape(chosen.shape[0], group_size * BLK)
            columns.append(
                lax.dot_general(
                    member_part, onehot_table, contract, preferred_element_type=jnp.float32
                )
            )
        gram_pieces.append(jnp.concatenate(columns, axis=1))
    gram_list = [jnp.concatenate(gram_pieces, axis=0)]
    return (jnp.stack(updated_list), jnp.stack(gram_list))


def solution(mesh):
    in_specs = (P("ingest", None), P(None, "ingest"), P("codes", "ingest", None), P())
    out_specs = (P("codes", "ingest", None), P("codes", "ingest", None))
    part = two_books if mesh.shape["codes"] == 2 else shards
    return jax.shard_map(part, mesh=mesh, in_specs=in_specs, out_specs=out_specs, check_vma=False)
```

```python
import functools

import jax
import jax.numpy as jnp
from jax import lax
from jax.experimental import pallas as pl
from jax.experimental.pallas import tpu as pltpu
from jax.sharding import PartitionSpec as P

K = 4096
BLK = 128
P_SIZE = 64
KB = 32
CHUNKS = 4
PLANE = 4
MESH = pl.DeviceIdType.MESH
VMEM_BYTES = 32 * 1024 * 1024


def whole(ref, sem):
    return pltpu.make_async_copy(ref, ref, sem)


def exchange_kernel(
    n, own, cap,
    codes_hbm, vec_hbm, book_hbm, pairs_hbm,
    got_ref, table_ref, member_ref, book_ref, pairs_out,
    codes_ref, vec_ref, allc, picks, ret, send, table, merge, cast,
    code_send, code_recv, one_send, one_recv, two_send, two_recv, local_sem,
    cast_near, cast_far, cast_on, cast_recv, in_sem,
):
    me = lax.axis_index("ingest")
    book = lax.axis_index("codes")
    other = 1 - book
    rows, dim = vec_ref.shape
    half = dim // 2
    width = half // CHUNKS
    slots = n * cap
    planes = n // PLANE
    plane = me // PLANE
    place = me % PLANE
    peers = 2 * PLANE
    my_peer = book * PLANE + place
    near = plane + 1 - 2 * (plane % 2)
    far = 2 - plane // 2
    f32, bf16, i32 = jnp.float32, jnp.bfloat16, jnp.int32

    load_codes = pltpu.make_async_copy(codes_hbm, codes_ref, in_sem.at[0])
    load_codes.start()
    load_book = pltpu.make_async_copy(book_hbm, book_ref, in_sem.at[1])
    load_book.start()
    load_vectors = pltpu.make_async_copy(vec_hbm, vec_ref, in_sem.at[2])
    load_vectors.start()
    load_pairs = pltpu.make_async_copy(pairs_hbm, pairs_out, in_sem.at[3])
    load_pairs.start()

    barrier = pltpu.get_barrier_semaphore()

    def greet(step, carry):
        peer = lax.rem(me + step, n)
        pl.semaphore_signal(barrier, inc=1, device_id=(peer, book), device_id_type=MESH)
        pl.semaphore_signal(barrier, inc=1, device_id=(peer, other), device_id_type=MESH)
        return carry

    pl.semaphore_signal(barrier, inc=1, device_id=(me, other), device_id_type=MESH)
    lax.fori_loop(1, n, greet, 0)
    load_codes.wait()
    pl.semaphore_wait(barrier, 2 * n - 1)

    def code_copy(step):
        peer = lax.rem(me + step, n)
        return pltpu.make_async_remote_copy(
            src_ref=codes_ref,
            dst_ref=allc.at[place * planes + plane],
            send_sem=code_send.at[step],
            recv_sem=code_recv.at[place * planes + plane],
            device_id=(peer, book),
            device_id_type=MESH,
        )

    def start_codes(step, carry):
        code_copy(step).start()
        return carry

    lax.fori_loop(1, n, start_codes, 0)
    earlier = (
        lax.broadcasted_iota(i32, (rows, rows), 0) < lax.broadcasted_iota(i32, (rows, rows), 1)
    ).astype(bf16)
    allc[place * planes + plane] = codes_ref[...]

    def wait_codes(step, carry):
        peer = lax.rem(me + step, n)
        source = peer % PLANE * planes + peer // PLANE
        whole(allc.at[source], code_recv.at[source]).wait()
        return carry

    lax.fori_loop(1, n, wait_codes, 0)

    all_codes = allc[...]
    firsts, seconds = all_codes[:, 0, :], all_codes[:, 1, :]
    own_all = jnp.where(book == 0, firsts, seconds)
    oth_all = jnp.where(book == 0, seconds, firsts)
    local = own_all - me * own
    inside = (local >= 0) & (local < own)
    before = jnp.dot(
        jnp.where(inside, 1.0, 0.0).astype(bf16), earlier, preferred_element_type=f32
    )
    rank = jnp.where(inside, before, -1.0).astype(i32)
    chosen = rank[:, None, :] == lax.broadcasted_iota(i32, (n, cap, rows), 1)
    local_one = (local + 1).astype(f32)
    row_code = jnp.sum(jnp.where(chosen, local_one[:, None, :], 0.0), axis=2, keepdims=True)
    row_code = row_code.reshape(slots, 1).astype(i32) - 1
    member32 = (row_code == lax.broadcasted_iota(i32, (slots, own), 1)).astype(f32)
    member = member32.astype(bf16)
    load_book.wait()

    def plane_copy(step, c, source, target, send_sem, recv_sem):
        q = lax.rem(my_peer + step, peers)
        return pltpu.make_async_remote_copy(
            src_ref=source.at[c, q],
            dst_ref=target.at[c, my_peer],
            send_sem=send_sem.at[c],
            recv_sem=recv_sem.at[c],
            device_id=(plane * PLANE + q % PLANE, q // PLANE),
            device_id_type=MESH,
        )

    def plane_start(c, source, target, send_sem, recv_sem, own_sem):
        def start(step, carry):
            plane_copy(step, c, source, target, send_sem, recv_sem).start()
            return carry

        lax.fori_loop(1, peers, start, 0)
        pltpu.make_async_copy(source.at[c, my_peer], target.at[c, my_peer], own_sem).start()

    def plane_wait(c, source, target, recv_sem, own_sem):
        pltpu.make_async_copy(source.at[c, my_peer], target.at[c, my_peer], own_sem).wait()
        whole(target.at[c, pl.ds(0, peers - 1)], recv_sem.at[c]).wait()

    def row_copy(step, c, core):
        peer = lax.rem(me + step, n)
        return pltpu.make_async_remote_copy(
            src_ref=picks.at[c, core, peer % PLANE, peer // PLANE],
            dst_ref=ret.at[c, book * n + me],
            send_sem=one_send.at[c],
            recv_sem=one_recv.at[c],
            device_id=(peer, core),
            device_id_type=MESH,
        )

    def own_rows(c):
        return pltpu.make_async_copy(
            picks.at[c, book, place, plane], ret.at[c, book * n + me], local_sem.at[0, c]
        )

    for c in range(CHUNKS):
        for core in range(2):
            at = core * half + c * width
            part = jnp.dot(member, book_ref[:, at : at + width], preferred_element_type=f32)
            picks[c, core] = part.astype(bf16).reshape(PLANE, planes, cap, width)

        def start_rows(step, carry):
            row_copy(step, c, 0).start()
            row_copy(step, c, 1).start()
            return carry

        lax.fori_loop(1, n, start_rows, 0)
        row_copy(0, c, other).start()
        own_rows(c).start()

    parts = []
    for m in range(2):
        code = codes_ref[m : m + 1, :]
        target = code // own
        hits = (target == lax.broadcasted_iota(i32, (n, rows), 0)).astype(f32)
        ahead = jnp.dot(hits.astype(bf16), earlier, preferred_element_type=f32)
        rank_row = jnp.sum(ahead * hits, axis=0, keepdims=True).astype(i32)
        slot = target * cap + rank_row
        parts.append((slot == lax.broadcasted_iota(i32, (slots, rows), 0)).astype(f32))
    merge[...] = jnp.transpose(jnp.concatenate(parts, axis=0)).astype(bf16)

    column = allc[pl.ds(place * planes, planes)]
    for d in range(planes):
        parts = []
        for m in range(2):
            code = column[d, m : m + 1, :]
            target = code // own
            hits = (target == lax.broadcasted_iota(i32, (n, rows), 0)).astype(f32)
            ahead = jnp.dot(hits.astype(bf16), earlier, preferred_element_type=f32)
            rank_row = jnp.sum(ahead * hits, axis=0, keepdims=True).astype(i32)
            slot = (target - plane * PLANE) * cap + rank_row
            inner = lax.broadcasted_iota(i32, (PLANE * cap, rows), 0)
            parts.append((slot == inner).astype(f32))
        table[d] = jnp.concatenate(parts, axis=0).astype(bf16)

    oth_one = (oth_all + 1).astype(f32)
    oth_slot = jnp.sum(jnp.where(chosen, oth_one[:, None, :], 0.0), axis=2, keepdims=True)
    oth_slot = oth_slot.reshape(slots, 1).astype(i32) - 1
    member_ref[...] = jnp.transpose(member32).astype(bf16)
    group = 4

    def count_pairs(q, carry):
        columns = lax.broadcasted_iota(i32, (slots, group * BLK), 1) + q * (group * BLK)
        onehot = (oth_slot == columns).astype(f32).astype(bf16)
        counts = jnp.dot(member_ref[...], onehot, preferred_element_type=f32)
        for i in range(group):
            table_ref[q * group + i] = counts[:, i * BLK : (i + 1) * BLK]
        return carry

    def near_copy(c):
        return pltpu.make_async_remote_copy(
            src_ref=cast.at[c, plane], dst_ref=cast.at[c, plane],
            send_sem=cast_near.at[c], recv_sem=cast_recv.at[c, plane],
            device_id=(near * PLANE + place, book), device_id_type=MESH,
        )

    def far_copy(c):
        return pltpu.make_async_remote_copy(
            src_ref=cast.at[c, plane], dst_ref=cast.at[c, plane],
            send_sem=cast_far.at[c], recv_sem=cast_recv.at[c, plane],
            device_id=(far * PLANE + place, book), device_id_type=MESH,
        )

    def on_copy(c, k):
        source = (1 - plane // 2) * 2 + k
        return pltpu.make_async_remote_copy(
            src_ref=cast.at[c, source], dst_ref=cast.at[c, source],
            send_sem=cast_on.at[c, k], recv_sem=cast_recv.at[c, source],
            device_id=(near * PLANE + place, book), device_id_type=MESH,
        )

    gateway = (plane == 1) | (plane == 2)

    def wait_cast(c, source):
        whole(cast.at[c, source], cast_recv.at[c, source]).wait()

    def residual_step(c):
        own_rows(c).wait()
        whole(ret.at[c, pl.ds(0, 2 * n - 1)], one_recv.at[c]).wait()
        rows_in = ret[c].reshape(2 * slots, width)
        recon = jnp.dot(merge[...], rows_in, preferred_element_type=f32)
        low = vec_ref[:, c * width : (c + 1) * width].astype(f32)
        high = vec_ref[:, half + c * width : half + (c + 1) * width].astype(f32)
        cast[c, plane] = (jnp.where(book == 0, low, high) - recon).astype(bf16)
        far_copy(c).start()
        near_copy(c).start()

    def hand_on_step(c):
        @pl.when(gateway)
        def _():
            for k in range(2):
                wait_cast(c, (1 - plane // 2) * 2 + k)
                on_copy(c, k).start()

    def spread_step(c):
        wait_cast(c, near)

        @pl.when(jnp.logical_not(gateway))
        def _():
            for k in range(2):
                wait_cast(c, (1 - plane // 2) * 2 + k)

        for d in range(planes):
            part = jnp.dot(table[d], cast[c, d], preferred_element_type=f32)
            send[c, :, d] = part.astype(bf16).reshape(peers, cap, width)
        plane_start(c, send, got_ref, two_send, two_recv, local_sem.at[1, c])

    load_vectors.wait()
    load_pairs.wait()
    per_chunk = KB // group // CHUNKS
    for t in range(CHUNKS):
        residual_step(t)
        lax.fori_loop(t * per_chunk, (t + 1) * per_chunk, count_pairs, 0)
        hand_on_step(t)
        if t >= 1:
            spread_step(t - 1)
    spread_step(CHUNKS - 1)

    def wait_code_sends(step, carry):
        code_copy(step).wait_send()
        return carry

    lax.fori_loop(1, n, wait_code_sends, 0)
    for c in range(CHUNKS):
        whole(ret.at[c, pl.ds(0, 2 * n - 1)], one_send.at[c]).wait()
        whole(send.at[c, pl.ds(0, peers - 1)], two_send.at[c]).wait()
        near_copy(c).wait_send()
        far_copy(c).wait_send()

        @pl.when(gateway)
        def _():
            on_copy(c, 0).wait_send()
            on_copy(c, 1).wait_send()

        plane_wait(c, send, got_ref, two_recv, local_sem.at[1, c])


def finish_kernel(
    pieces, pairs_in, got_ref, member_ref, table_ref, book_ref, new_ref, gram_ref, pairs_ref, newv, sems
):
    me = lax.axis_index("ingest")
    book = lax.axis_index("codes")
    first_row = book * KB + me * pieces
    other_start = (1 - book) * KB
    load = pltpu.make_async_copy(pairs_in, pairs_ref, sems.at[0])
    load.start()
    f32 = jnp.float32
    member = member_ref[...]
    load.wait()

    for piece in range(pieces):

        def place(p, carry):
            block = pairs_ref[first_row + piece, p] - other_start
            pltpu.make_async_copy(
                table_ref.at[block, pl.ds(piece * BLK, BLK)],
                gram_ref.at[0, pl.ds(piece * BLK, BLK), pl.ds(pl.multiple_of(p * BLK, BLK), BLK)],
                sems.at[1],
            ).start()
            return carry

        lax.fori_loop(0, P_SIZE, place, 0, unroll=8)

    count = jnp.sum(member.astype(f32), axis=1, keepdims=True)
    scale = 1.0 / (count + 2.0)
    slots = member.shape[1]
    width = got_ref.shape[-1]
    half = CHUNKS * width
    for c in range(CHUNKS):
        for core in range(2):
            rows_in = got_ref[c, core * PLANE : (core + 1) * PLANE].reshape(slots, width)
            total = jnp.dot(member, rows_in, preferred_element_type=f32)
            at = core * half + c * width
            current = book_ref[:, at : at + width].astype(f32)
            newv[0, :, at : at + width] = current + (total - 2.0 * current) * scale
    store = pltpu.make_async_copy(newv, new_ref, sems.at[0])
    store.start()
    store.wait()
    whole(gram_ref, sems.at[1]).wait()


def two_books(vectors, codes, codebook, pairs):
    n = lax.axis_size("ingest")
    rows, dim = vectors.shape
    own = codebook.shape[1]
    cap = 2 * rows // n
    slots = n * cap
    planes = n // PLANE
    width = dim // 2 // CHUNKS
    f32, bf16, i32 = jnp.float32, jnp.bfloat16, jnp.int32
    vmem = pl.BlockSpec(memory_space=pltpu.VMEM)
    hbm = pl.BlockSpec(memory_space=pltpu.HBM)
    dma = pltpu.SemaphoreType.DMA
    block = (CHUNKS, 2 * PLANE, planes, cap, width)
    dense = (CHUNKS, planes, rows, width)
    per_chunk = dma((CHUNKS,))
    held = [
        pltpu.with_memory_space_constraint(x, pltpu.HBM)
        for x in (codes, vectors, codebook[0], pairs)
    ]
    got, table, member, book, pairs = pl.pallas_call(
        functools.partial(exchange_kernel, n, own, cap),
        out_shape=(
            jax.ShapeDtypeStruct(block, bf16),
            jax.ShapeDtypeStruct((KB, own, BLK), f32),
            jax.ShapeDtypeStruct((own, slots), bf16),
            jax.ShapeDtypeStruct((own, dim), bf16),
            jax.ShapeDtypeStruct(pairs.shape, i32),
        ),
        in_specs=[hbm] * 4,
        out_specs=(vmem,) * 5,
        scratch_shapes=[
            pltpu.VMEM(codes.shape, i32),
            pltpu.VMEM((rows, dim), bf16),
            pltpu.VMEM((n,) + codes.shape, i32),
            pltpu.VMEM((CHUNKS, 2, PLANE, planes, cap, width), bf16),
            pltpu.VMEM((CHUNKS, 2 * n, cap, width), bf16),
            pltpu.VMEM(block, bf16),
            pltpu.VMEM((planes, 2 * PLANE * cap, rows), bf16),
            pltpu.VMEM((rows, 2 * slots), bf16),
            pltpu.VMEM(dense, bf16),
            dma((n,)),
            dma((n,)),
            per_chunk,
            per_chunk,
            per_chunk,
            per_chunk,
            dma((2, CHUNKS)),
            per_chunk,
            per_chunk,
            dma((CHUNKS, 2)),
            dma((CHUNKS, planes)),
            dma((4,)),
        ],
        compiler_params=pltpu.CompilerParams(
            collective_id=0, has_side_effects=True, vmem_limit_bytes=VMEM_BYTES
        ),
        name="exchange",
    )(*held)
    return pl.pallas_call(
        functools.partial(finish_kernel, own // BLK),
        out_shape=(
            jax.ShapeDtypeStruct((1, own, dim), f32),
            jax.ShapeDtypeStruct((1, own, P_SIZE * BLK), f32),
        ),
        in_specs=[vmem] * 5,
        out_specs=(hbm, hbm),
        scratch_shapes=[
            pltpu.SMEM(pairs.shape, i32),
            pltpu.VMEM((1, own, dim), f32),
            dma((2,)),
        ],
        compiler_params=pltpu.CompilerParams(vmem_limit_bytes=16 * 1024 * 1024),
        name="finish",
    )(pairs, got, member, table, book)


def shards(vectors, codes, codebook, pairs):
    owners = lax.axis_size("ingest")
    my_owner = lax.axis_index("ingest")
    my_group = lax.axis_index("codes")
    rows_count = vectors.shape[0]
    books_dev = codebook.shape[0]
    own_rows = codebook.shape[1]
    feature_dim = codebook.shape[2]
    codebooks = codes.shape[0]
    capacity = 2 * rows_count // owners
    slot_total = owners * books_dev * capacity
    local_codes = lax.dynamic_slice_in_dim(codes, my_group * books_dev, books_dev, 0)
    target = local_codes // own_rows
    within = local_codes - target * own_rows
    owner_hits = (target[:, :, None] == jnp.arange(owners, dtype=jnp.int32)).astype(jnp.int32)
    before = jnp.cumsum(owner_hits, axis=1) - owner_hits
    slot_rank = jnp.sum(before * owner_hits, axis=2)
    book_offset = jnp.arange(books_dev, dtype=jnp.int32)[:, None]
    slot_index = (target * books_dev + book_offset) * capacity + slot_rank
    slot_flat = slot_index.reshape(-1)
    vector_ids = jnp.broadcast_to(
        jnp.arange(rows_count, dtype=jnp.int32), (books_dev, rows_count)
    ).reshape(-1)
    slot_vector = jnp.full((slot_total,), rows_count, jnp.int32).at[slot_flat].set(vector_ids)
    asked_rows = (within + book_offset * own_rows).reshape(-1)
    slot_request = jnp.full((slot_total,), -1, jnp.int32).at[slot_flat].set(asked_rows)
    slot_request = slot_request.reshape(owners, books_dev * capacity)
    flat_book = codebook.reshape(books_dev * own_rows, feature_dim)
    picked = jnp.take(
        flat_book,
        jnp.maximum(
            lax.all_to_all(slot_request, "ingest", split_axis=0, concat_axis=0, tiled=True), 0
        ),
        axis=0,
    )
    returned = lax.all_to_all(picked, "ingest", split_axis=0, concat_axis=0, tiled=True)
    fetched = jnp.take(returned.reshape(slot_total, feature_dim), slot_index, axis=0)
    partial_sum = jnp.sum(fetched.astype(jnp.float32), axis=0)
    full_sum = lax.psum(partial_sum.astype(jnp.bfloat16), "codes").astype(jnp.float32)
    residual = (vectors.astype(jnp.float32) - full_sum).astype(jnp.bfloat16)
    residual_ext = jnp.concatenate([residual, jnp.zeros((1, feature_dim), jnp.bfloat16)], axis=0)
    codes_ext = jnp.concatenate([codes.T, jnp.full((1, codebooks), -1, jnp.int32)], axis=0)
    send_rows = jnp.take(residual_ext, slot_vector, axis=0).reshape(
        owners, books_dev * capacity, feature_dim
    )
    send_codes = jnp.take(codes_ext, slot_vector, axis=0).reshape(
        owners, books_dev * capacity, codebooks
    )
    got_rows, got_codes = (
        lax.all_to_all(send_rows, "ingest", split_axis=0, concat_axis=0, tiled=True),
        lax.all_to_all(send_codes, "ingest", split_axis=0, concat_axis=0, tiled=True),
    )
    got_rows = got_rows.reshape(owners, books_dev, capacity, feature_dim)
    got_codes = got_codes.reshape(owners, books_dev, capacity, codebooks)
    block_rows = min(own_rows, BLK)
    pieces = own_rows // block_rows
    group_size = min(P_SIZE, 8)
    contract = (((0,), (0,)), ((), ()))
    rows_in = got_rows[:, 0].reshape(owners * capacity, feature_dim)
    tuples = got_codes[:, 0].reshape(owners * capacity, codebooks)
    book_global = my_group * books_dev + 0
    own_code = lax.dynamic_index_in_dim(tuples, book_global, 1, keepdims=False)
    local_row = own_code - my_owner * own_rows
    member = (local_row[:, None] == jnp.arange(own_rows, dtype=jnp.int32)).astype(jnp.bfloat16)
    right_side = lax.dot_general(member, rows_in, contract, preferred_element_type=jnp.float32)
    code_count = jnp.sum(member, axis=0, dtype=jnp.float32)
    current = codebook[0].astype(jnp.float32)
    updated_list = [current + (right_side - 2.0 * current) / (code_count[:, None] + 2.0)]
    gram_pieces = []
    for part_index in range(pieces):
        first_row = book_global * K + my_owner * own_rows + part_index * block_rows
        partner = lax.dynamic_index_in_dim(pairs, first_row // BLK, 0, keepdims=False)
        partner_book = partner // KB
        partner_start = partner % KB * BLK
        partner_code = jnp.take(tuples, partner_book, axis=1) - partner_start[None, :]
        member_part = member[:, part_index * block_rows : (part_index + 1) * block_rows]
        columns = []
        for group_index in range(P_SIZE // group_size):
            chosen = partner_code[:, group_index * group_size : (group_index + 1) * group_size]
            onehot_table = (chosen[:, :, None] == jnp.arange(BLK, dtype=jnp.int32)).astype(
                jnp.bfloat16
            )
            onehot_table = onehot_table.reshape(chosen.shape[0], group_size * BLK)
            columns.append(
                lax.dot_general(
                    member_part, onehot_table, contract, preferred_element_type=jnp.float32
                )
            )
        gram_pieces.append(jnp.concatenate(columns, axis=1))
    gram_list = [jnp.concatenate(gram_pieces, axis=0)]
    return (jnp.stack(updated_list), jnp.stack(gram_list))


def solution(mesh):
    in_specs = (P("ingest", None), P(None, "ingest"), P("codes", "ingest", None), P())
    out_specs = (P("codes", "ingest", None), P("codes", "ingest", None))
    part = two_books if dict(mesh.shape) == {"ingest": 4 * PLANE, "codes": 2} else shards
    return jax.shard_map(part, mesh=mesh, in_specs=in_specs, out_specs=out_specs, check_vma=False)
```

```python
import functools

import jax
import jax.numpy as jnp
from jax import lax
from jax.experimental import pallas as pl
from jax.experimental.pallas import tpu as pltpu
from jax.sharding import PartitionSpec as P

K = 4096
BLK = 128
P_SIZE = 64
KB = 32
CHUNKS = 2
MESH = pl.DeviceIdType.MESH
VMEM_BYTES = 32 * 1024 * 1024


PLANE = 4


def flipped(x, k):
    low = x % 4
    if k == 1:
        return x + 1 - 2 * (low % 2)
    if k == 2:
        return x - low + (low + 2) % 4
    if k == 3:
        return x - low + 3 - low
    return x


def partners(me, n):
    order = []
    planes = n // PLANE
    for base in range(0, planes, 4):
        for k in (2, 3, 1, 0):
            for j in range(PLANE):
                if base or k or j:
                    plane = me // PLANE
                    peer = flipped(plane, k) if planes % 4 == 0 else plane
                    peer = (peer + base) % planes
                    order.append(peer * PLANE + flipped(me % PLANE, j))
    return order


def whole(ref, sem):
    return pltpu.make_async_copy(ref, ref, sem)


def exchange_kernel(
    n, own, cap,
    codes_hbm, vec_hbm, book_hbm, pairs_hbm,
    got_ref, table_ref, member_ref, pairs_out,
    codes_ref, vec_ref, book_ref, allc, picks, ret, send,
    code_send, code_recv, one_send, one_recv, two_send, two_recv, local_sem, in_sem,
):
    me = lax.axis_index("ingest")
    book = lax.axis_index("codes")
    other = 1 - book
    rows, dim = vec_ref.shape
    width = dim // CHUNKS
    slots = n * cap
    f32, bf16, i32 = jnp.float32, jnp.bfloat16, jnp.int32

    load_codes = pltpu.make_async_copy(codes_hbm, codes_ref, in_sem.at[0])
    load_codes.start()
    load_book = pltpu.make_async_copy(book_hbm, book_ref, in_sem.at[1])
    load_book.start()
    load_vectors = pltpu.make_async_copy(vec_hbm, vec_ref, in_sem.at[2])
    load_vectors.start()
    load_pairs = pltpu.make_async_copy(pairs_hbm, pairs_out, in_sem.at[3])
    load_pairs.start()

    barrier = pltpu.get_barrier_semaphore()

    def greet(step, carry):
        peer = lax.rem(me + step, n)
        pl.semaphore_signal(barrier, inc=1, device_id=(peer, book), device_id_type=MESH)
        pl.semaphore_signal(barrier, inc=1, device_id=(peer, other), device_id_type=MESH)
        return carry

    pl.semaphore_signal(barrier, inc=1, device_id=(me, other), device_id_type=MESH)
    lax.fori_loop(1, n, greet, 0)
    load_codes.wait()
    pl.semaphore_wait(barrier, 2 * n - 1)

    def code_copy(step):
        peer = lax.rem(me + step, n)
        return pltpu.make_async_remote_copy(
            src_ref=codes_ref,
            dst_ref=allc.at[me],
            send_sem=code_send.at[step],
            recv_sem=code_recv.at[me],
            device_id=(peer, book),
            device_id_type=MESH,
        )

    def start_codes(step, carry):
        code_copy(step).start()
        return carry

    lax.fori_loop(1, n, start_codes, 0)

    earlier = (
        lax.broadcasted_iota(i32, (rows, rows), 0) < lax.broadcasted_iota(i32, (rows, rows), 1)
    ).astype(bf16)
    mine = codes_ref[...]
    first, second = mine[0:1, :], mine[1:2, :]
    own_code = jnp.where(book == 0, first, second)
    oth_code = jnp.where(book == 0, second, first)

    def slot_table(code):
        target = code // own
        hits = (target == lax.broadcasted_iota(i32, (n, rows), 0)).astype(f32)
        before = jnp.dot(hits.astype(bf16), earlier, preferred_element_type=f32)
        rank = jnp.sum(before * hits, axis=0, keepdims=True)
        slot = target * cap + rank.astype(i32)
        return (slot == lax.broadcasted_iota(i32, (slots, rows), 0)).astype(f32)

    allc[me] = mine

    def wait_codes(step, carry):
        source = lax.rem(me + step, n)
        whole(allc.at[source], code_recv.at[source]).wait()
        return carry

    lax.fori_loop(1, n, wait_codes, 0)

    all_codes = allc[...]
    firsts, seconds = all_codes[:, 0, :], all_codes[:, 1, :]
    own_all = jnp.where(book == 0, firsts, seconds)
    oth_all = jnp.where(book == 0, seconds, firsts)
    local = own_all - me * own
    inside = (local >= 0) & (local < own)
    before = jnp.dot(
        jnp.where(inside, 1.0, 0.0).astype(bf16), earlier, preferred_element_type=f32
    )
    rank = jnp.where(inside, before, -1.0).astype(i32)
    chosen = rank[:, None, :] == lax.broadcasted_iota(i32, (n, cap, rows), 1)
    local_one = (local + 1).astype(f32)
    row_code = jnp.sum(jnp.where(chosen, local_one[:, None, :], 0.0), axis=2, keepdims=True)
    row_code = row_code.reshape(slots, 1).astype(i32) - 1
    member32 = (row_code == lax.broadcasted_iota(i32, (slots, own), 1)).astype(f32)
    member = member32.astype(bf16)

    load_book.wait()

    others = partners(me, n)

    def start_one(c):
        part = jnp.dot(
            member, book_ref[:, c * width : (c + 1) * width], preferred_element_type=f32
        )
        picks[c] = part.astype(bf16).reshape(n, cap, width)
        for peer in others + [me]:
            pltpu.make_async_remote_copy(
                src_ref=picks.at[c, peer],
                dst_ref=ret.at[c, me],
                send_sem=one_send.at[c],
                recv_sem=one_recv.at[c],
                device_id=(peer, other),
                device_id_type=MESH,
            ).start()

    start_one(0)

    send_table = slot_table(own_code).astype(bf16)
    merge_table = jnp.transpose(slot_table(oth_code)).astype(bf16)

    oth_one = (oth_all + 1).astype(f32)
    oth_slot = jnp.sum(jnp.where(chosen, oth_one[:, None, :], 0.0), axis=2, keepdims=True)
    oth_slot = oth_slot.reshape(slots, 1).astype(i32) - 1
    member_ref[...] = jnp.transpose(member32).astype(bf16)
    group = 4

    def count_pairs(q, carry):
        columns = lax.broadcasted_iota(i32, (slots, group * BLK), 1) + q * (group * BLK)
        onehot = (oth_slot == columns).astype(f32).astype(bf16)
        counts = jnp.dot(member_ref[...], onehot, preferred_element_type=f32)
        for i in range(group):
            table_ref[q * group + i] = counts[:, i * BLK : (i + 1) * BLK]
        return carry

    lax.fori_loop(0, KB // group, count_pairs, 0)
    for c in range(1, CHUNKS):
        start_one(c)
    load_vectors.wait()
    load_pairs.wait()

    for c in range(CHUNKS):
        whole(ret.at[c], one_recv.at[c]).wait()
        rows_in = ret[c].reshape(slots, width)
        fetched = jnp.dot(merge_table, rows_in, preferred_element_type=f32)
        target = vec_ref[:, c * width : (c + 1) * width].astype(f32) - fetched
        part = jnp.dot(send_table, target.astype(bf16), preferred_element_type=f32)
        send[c] = part.astype(bf16).reshape(n, cap, width)

        for peer in others:
            pltpu.make_async_remote_copy(
                src_ref=send.at[c, peer],
                dst_ref=got_ref.at[c, me],
                send_sem=two_send.at[c],
                recv_sem=two_recv.at[c],
                device_id=(peer, book),
                device_id_type=MESH,
            ).start()
        pltpu.make_async_copy(send.at[c, me], got_ref.at[c, me], local_sem.at[c]).start()

    def wait_code_sends(step, carry):
        code_copy(step).wait_send()
        return carry

    lax.fori_loop(1, n, wait_code_sends, 0)
    for c in range(CHUNKS):
        whole(picks.at[c], one_send.at[c]).wait()
        whole(send.at[c, pl.ds(0, n - 1)], two_send.at[c]).wait()
        pltpu.make_async_copy(send.at[c, me], got_ref.at[c, me], local_sem.at[c]).wait()
        whole(got_ref.at[c, pl.ds(0, n - 1)], two_recv.at[c]).wait()


def finish_kernel(
    pieces, pairs_in, got_ref, member_ref, table_ref, new_ref, gram_ref, pairs_ref, newv, sems
):
    me = lax.axis_index("ingest")
    book = lax.axis_index("codes")
    first_row = book * KB + me * pieces
    other_start = (1 - book) * KB
    load = pltpu.make_async_copy(pairs_in, pairs_ref, sems.at[0])
    load.start()
    f32 = jnp.float32
    member = member_ref[...]
    load.wait()

    for piece in range(pieces):

        def place(p, carry):
            block = pairs_ref[first_row + piece, p] - other_start
            pltpu.make_async_copy(
                table_ref.at[block, pl.ds(piece * BLK, BLK)],
                gram_ref.at[0, pl.ds(piece * BLK, BLK), pl.ds(pl.multiple_of(p * BLK, BLK), BLK)],
                sems.at[1],
            ).start()
            return carry

        lax.fori_loop(0, P_SIZE, place, 0)

    count = jnp.sum(member.astype(f32), axis=1, keepdims=True)
    scale = 1.0 / (count + 2.0)
    slots = member.shape[1]
    width = got_ref.shape[-1]
    for c in range(CHUNKS):
        rows_in = got_ref[c].reshape(slots, width)
        total = jnp.dot(member, rows_in, preferred_element_type=f32)
        newv[0, :, c * width : (c + 1) * width] = total * scale
    store = pltpu.make_async_copy(newv, new_ref, sems.at[0])
    store.start()
    store.wait()
    whole(gram_ref, sems.at[1]).wait()


def two_books(vectors, codes, codebook, pairs):
    n = lax.axis_size("ingest")
    rows, dim = vectors.shape
    own = codebook.shape[1]
    cap = 2 * rows // n
    slots = n * cap
    width = dim // CHUNKS
    f32, bf16 = jnp.float32, jnp.bfloat16
    vmem = pl.BlockSpec(memory_space=pltpu.VMEM)
    hbm = pl.BlockSpec(memory_space=pltpu.HBM)
    dma = pltpu.SemaphoreType.DMA
    block = (CHUNKS, n, cap, width)
    got, table, member, pairs = pl.pallas_call(
        functools.partial(exchange_kernel, n, own, cap),
        out_shape=(
            jax.ShapeDtypeStruct(block, bf16),
            jax.ShapeDtypeStruct((KB, own, BLK), f32),
            jax.ShapeDtypeStruct((own, slots), bf16),
            jax.ShapeDtypeStruct(pairs.shape, jnp.int32),
        ),
        in_specs=[hbm] * 4,
        out_specs=(vmem,) * 4,
        scratch_shapes=[
            pltpu.VMEM(codes.shape, jnp.int32),
            pltpu.VMEM((rows, dim), bf16),
            pltpu.VMEM((own, dim), bf16),
            pltpu.VMEM((n,) + codes.shape, jnp.int32),
            pltpu.VMEM(block, bf16),
            pltpu.VMEM(block, bf16),
            pltpu.VMEM(block, bf16),
            dma((n,)),
            dma((n,)),
            dma((CHUNKS,)),
            dma((CHUNKS,)),
            dma((CHUNKS,)),
            dma((CHUNKS,)),
            dma((CHUNKS,)),
            dma((4,)),
        ],
        compiler_params=pltpu.CompilerParams(
            collective_id=0, has_side_effects=True, vmem_limit_bytes=VMEM_BYTES
        ),
        name="exchange",
    )(*(pltpu.with_memory_space_constraint(a, pltpu.HBM) for a in (codes, vectors, codebook[0], pairs)))
    return pl.pallas_call(
        functools.partial(finish_kernel, own // BLK),
        out_shape=(
            jax.ShapeDtypeStruct((1, own, dim), f32),
            jax.ShapeDtypeStruct((1, own, P_SIZE * BLK), f32),
        ),
        in_specs=[vmem] * 4,
        out_specs=(hbm, hbm),
        scratch_shapes=[
            pltpu.SMEM(pairs.shape, jnp.int32),
            pltpu.VMEM((1, own, dim), f32),
            dma((2,)),
        ],
        compiler_params=pltpu.CompilerParams(vmem_limit_bytes=16 * 1024 * 1024),
        name="finish",
    )(pairs, got, member, table)


def shards(vectors, codes, codebook, pairs):
    owners = lax.axis_size("ingest")
    my_owner = lax.axis_index("ingest")
    my_group = lax.axis_index("codes")
    rows_count = vectors.shape[0]
    books_dev = codebook.shape[0]
    own_rows = codebook.shape[1]
    feature_dim = codebook.shape[2]
    codebooks = codes.shape[0]
    capacity = 2 * rows_count // owners
    slot_total = owners * books_dev * capacity
    local_codes = lax.dynamic_slice_in_dim(codes, my_group * books_dev, books_dev, 0)
    target = local_codes // own_rows
    within = local_codes - target * own_rows
    owner_hits = (target[:, :, None] == jnp.arange(owners, dtype=jnp.int32)).astype(jnp.int32)
    before = jnp.cumsum(owner_hits, axis=1) - owner_hits
    slot_rank = jnp.sum(before * owner_hits, axis=2)
    book_offset = jnp.arange(books_dev, dtype=jnp.int32)[:, None]
    slot_index = (target * books_dev + book_offset) * capacity + slot_rank
    slot_flat = slot_index.reshape(-1)
    vector_ids = jnp.broadcast_to(
        jnp.arange(rows_count, dtype=jnp.int32), (books_dev, rows_count)
    ).reshape(-1)
    slot_vector = jnp.full((slot_total,), rows_count, jnp.int32).at[slot_flat].set(vector_ids)
    asked_rows = (within + book_offset * own_rows).reshape(-1)
    slot_request = jnp.full((slot_total,), -1, jnp.int32).at[slot_flat].set(asked_rows)
    slot_request = slot_request.reshape(owners, books_dev * capacity)
    flat_book = codebook.reshape(books_dev * own_rows, feature_dim)
    picked = jnp.take(
        flat_book,
        jnp.maximum(
            lax.all_to_all(slot_request, "ingest", split_axis=0, concat_axis=0, tiled=True), 0
        ),
        axis=0,
    )
    returned = lax.all_to_all(picked, "ingest", split_axis=0, concat_axis=0, tiled=True)
    fetched = jnp.take(returned.reshape(slot_total, feature_dim), slot_index, axis=0)
    partial_sum = jnp.sum(fetched.astype(jnp.float32), axis=0)
    full_sum = lax.psum(partial_sum.astype(jnp.bfloat16), "codes").astype(jnp.float32)
    residual = (vectors.astype(jnp.float32) - full_sum).astype(jnp.bfloat16)
    residual_ext = jnp.concatenate([residual, jnp.zeros((1, feature_dim), jnp.bfloat16)], axis=0)
    codes_ext = jnp.concatenate([codes.T, jnp.full((1, codebooks), -1, jnp.int32)], axis=0)
    send_rows = jnp.take(residual_ext, slot_vector, axis=0).reshape(
        owners, books_dev * capacity, feature_dim
    )
    send_codes = jnp.take(codes_ext, slot_vector, axis=0).reshape(
        owners, books_dev * capacity, codebooks
    )
    got_rows, got_codes = (
        lax.all_to_all(send_rows, "ingest", split_axis=0, concat_axis=0, tiled=True),
        lax.all_to_all(send_codes, "ingest", split_axis=0, concat_axis=0, tiled=True),
    )
    got_rows = got_rows.reshape(owners, books_dev, capacity, feature_dim)
    got_codes = got_codes.reshape(owners, books_dev, capacity, codebooks)
    block_rows = min(own_rows, BLK)
    pieces = own_rows // block_rows
    group_size = min(P_SIZE, 8)
    contract = (((0,), (0,)), ((), ()))
    rows_in = got_rows[:, 0].reshape(owners * capacity, feature_dim)
    tuples = got_codes[:, 0].reshape(owners * capacity, codebooks)
    book_global = my_group * books_dev + 0
    own_code = lax.dynamic_index_in_dim(tuples, book_global, 1, keepdims=False)
    local_row = own_code - my_owner * own_rows
    member = (local_row[:, None] == jnp.arange(own_rows, dtype=jnp.int32)).astype(jnp.bfloat16)
    right_side = lax.dot_general(member, rows_in, contract, preferred_element_type=jnp.float32)
    code_count = jnp.sum(member, axis=0, dtype=jnp.float32)
    current = codebook[0].astype(jnp.float32)
    updated_list = [current + (right_side - 2.0 * current) / (code_count[:, None] + 2.0)]
    gram_pieces = []
    for part_index in range(pieces):
        first_row = book_global * K + my_owner * own_rows + part_index * block_rows
        partner = lax.dynamic_index_in_dim(pairs, first_row // BLK, 0, keepdims=False)
        partner_book = partner // KB
        partner_start = partner % KB * BLK
        partner_code = jnp.take(tuples, partner_book, axis=1) - partner_start[None, :]
        member_part = member[:, part_index * block_rows : (part_index + 1) * block_rows]
        columns = []
        for group_index in range(P_SIZE // group_size):
            chosen = partner_code[:, group_index * group_size : (group_index + 1) * group_size]
            onehot_table = (chosen[:, :, None] == jnp.arange(BLK, dtype=jnp.int32)).astype(
                jnp.bfloat16
            )
            onehot_table = onehot_table.reshape(chosen.shape[0], group_size * BLK)
            columns.append(
                lax.dot_general(
                    member_part, onehot_table, contract, preferred_element_type=jnp.float32
                )
            )
        gram_pieces.append(jnp.concatenate(columns, axis=1))
    gram_list = [jnp.concatenate(gram_pieces, axis=0)]
    return (jnp.stack(updated_list), jnp.stack(gram_list))


def solution(mesh):
    in_specs = (P("ingest", None), P(None, "ingest"), P("codes", "ingest", None), P())
    out_specs = (P("codes", "ingest", None), P("codes", "ingest", None))
    part = two_books if dict(mesh.shape) == {"ingest": 4 * PLANE, "codes": 2} else shards
    return jax.shard_map(part, mesh=mesh, in_specs=in_specs, out_specs=out_specs, check_vma=False)
```

```python
import functools

import jax
import jax.numpy as jnp
from jax import lax
from jax.experimental import pallas as pl
from jax.experimental.pallas import tpu as pltpu
from jax.sharding import PartitionSpec as P

K = 4096
BLK = 128
P_SIZE = 64
KB = 32
CHUNKS = 2
MESH = pl.DeviceIdType.MESH
VMEM_BYTES = 32 * 1024 * 1024


def whole(ref, sem):
    return pltpu.make_async_copy(ref, ref, sem)


def exchange_kernel(
    n, own, cap,
    codes_hbm, vec_hbm, book_hbm, pairs_hbm,
    got_ref, table_ref, member_ref, pairs_out,
    codes_ref, vec_ref, book_ref, allc, picks, ret, send,
    code_send, code_recv, one_send, one_recv, two_send, two_recv, local_sem, in_sem,
):
    me = lax.axis_index("ingest")
    book = lax.axis_index("codes")
    other = 1 - book
    rows, dim = vec_ref.shape
    width = dim // CHUNKS
    slots = n * cap
    f32, bf16, i32 = jnp.float32, jnp.bfloat16, jnp.int32

    load_codes = pltpu.make_async_copy(codes_hbm, codes_ref, in_sem.at[0])
    load_codes.start()
    load_book = pltpu.make_async_copy(book_hbm, book_ref, in_sem.at[1])
    load_book.start()
    load_vectors = pltpu.make_async_copy(vec_hbm, vec_ref, in_sem.at[2])
    load_vectors.start()
    load_pairs = pltpu.make_async_copy(pairs_hbm, pairs_out, in_sem.at[3])
    load_pairs.start()

    barrier = pltpu.get_barrier_semaphore()

    def greet(step, carry):
        peer = lax.rem(me + step, n)
        pl.semaphore_signal(barrier, inc=1, device_id=(peer, book), device_id_type=MESH)
        pl.semaphore_signal(barrier, inc=1, device_id=(peer, other), device_id_type=MESH)
        return carry

    pl.semaphore_signal(barrier, inc=1, device_id=(me, other), device_id_type=MESH)
    lax.fori_loop(1, n, greet, 0)
    load_codes.wait()
    pl.semaphore_wait(barrier, 2 * n - 1)

    def code_copy(step):
        peer = lax.rem(me + step, n)
        return pltpu.make_async_remote_copy(
            src_ref=codes_ref,
            dst_ref=allc.at[me],
            send_sem=code_send.at[step],
            recv_sem=code_recv.at[me],
            device_id=(peer, book),
            device_id_type=MESH,
        )

    def start_codes(step, carry):
        code_copy(step).start()
        return carry

    lax.fori_loop(1, n, start_codes, 0)

    earlier = (
        lax.broadcasted_iota(i32, (rows, rows), 0) < lax.broadcasted_iota(i32, (rows, rows), 1)
    ).astype(bf16)
    mine = codes_ref[...]
    first, second = mine[0:1, :], mine[1:2, :]
    own_code = jnp.where(book == 0, first, second)
    oth_code = jnp.where(book == 0, second, first)

    def slot_table(code):
        target = code // own
        hits = (target == lax.broadcasted_iota(i32, (n, rows), 0)).astype(f32)
        before = jnp.dot(hits.astype(bf16), earlier, preferred_element_type=f32)
        rank = jnp.sum(before * hits, axis=0, keepdims=True)
        slot = target * cap + rank.astype(i32)
        return (slot == lax.broadcasted_iota(i32, (slots, rows), 0)).astype(f32)

    send_table = slot_table(own_code).astype(bf16)
    merge_table = jnp.transpose(slot_table(oth_code)).astype(bf16)

    allc[me] = mine

    def wait_codes(step, carry):
        source = lax.rem(me + step, n)
        whole(allc.at[source], code_recv.at[source]).wait()
        return carry

    lax.fori_loop(1, n, wait_codes, 0)

    all_codes = allc[...]
    firsts, seconds = all_codes[:, 0, :], all_codes[:, 1, :]
    own_all = jnp.where(book == 0, firsts, seconds)
    oth_all = jnp.where(book == 0, seconds, firsts)
    local = own_all - me * own
    inside = (local >= 0) & (local < own)
    before = jnp.dot(
        jnp.where(inside, 1.0, 0.0).astype(bf16), earlier, preferred_element_type=f32
    )
    rank = jnp.where(inside, before, -1.0).astype(i32)
    chosen = rank[:, None, :] == lax.broadcasted_iota(i32, (n, cap, rows), 1)
    local_one = (local + 1).astype(f32)
    row_code = jnp.sum(jnp.where(chosen, local_one[:, None, :], 0.0), axis=2, keepdims=True)
    row_code = row_code.reshape(slots, 1).astype(i32) - 1
    member32 = (row_code == lax.broadcasted_iota(i32, (slots, own), 1)).astype(f32)
    member = member32.astype(bf16)

    load_book.wait()

    for c in range(CHUNKS):
        part = jnp.dot(
            member, book_ref[:, c * width : (c + 1) * width], preferred_element_type=f32
        )
        picks[c] = part.astype(bf16).reshape(n, cap, width)

        def start_one(step, carry):
            peer = lax.rem(me + step, n)
            pltpu.make_async_remote_copy(
                src_ref=picks.at[c, peer],
                dst_ref=ret.at[c, me],
                send_sem=one_send.at[c],
                recv_sem=one_recv.at[c],
                device_id=(peer, other),
                device_id_type=MESH,
            ).start()
            return carry

        lax.fori_loop(0, n, start_one, 0)

    load_vectors.wait()
    load_pairs.wait()

    for c in range(CHUNKS):
        whole(ret.at[c], one_recv.at[c]).wait()
        rows_in = ret[c].reshape(slots, width)
        fetched = jnp.dot(merge_table, rows_in, preferred_element_type=f32)
        target = vec_ref[:, c * width : (c + 1) * width].astype(f32) - fetched
        part = jnp.dot(send_table, target.astype(bf16), preferred_element_type=f32)
        send[c] = part.astype(bf16).reshape(n, cap, width)

        def start_two(step, carry):
            peer = lax.rem(me + step, n)
            pltpu.make_async_remote_copy(
                src_ref=send.at[c, peer],
                dst_ref=got_ref.at[c, me],
                send_sem=two_send.at[c],
                recv_sem=two_recv.at[c],
                device_id=(peer, book),
                device_id_type=MESH,
            ).start()
            return carry

        lax.fori_loop(1, n, start_two, 0)
        pltpu.make_async_copy(send.at[c, me], got_ref.at[c, me], local_sem.at[c]).start()

    oth_one = (oth_all + 1).astype(f32)
    oth_slot = jnp.sum(jnp.where(chosen, oth_one[:, None, :], 0.0), axis=2, keepdims=True)
    oth_slot = oth_slot.reshape(slots, 1).astype(i32) - 1
    member_ref[...] = jnp.transpose(member32).astype(bf16)
    group = 4

    def count_pairs(q, carry):
        columns = lax.broadcasted_iota(i32, (slots, group * BLK), 1) + q * (group * BLK)
        onehot = (oth_slot == columns).astype(f32).astype(bf16)
        counts = jnp.dot(member_ref[...], onehot, preferred_element_type=f32)
        for i in range(group):
            table_ref[q * group + i] = counts[:, i * BLK : (i + 1) * BLK]
        return carry

    lax.fori_loop(0, KB // group, count_pairs, 0)
    def wait_code_sends(step, carry):
        code_copy(step).wait_send()
        return carry

    lax.fori_loop(1, n, wait_code_sends, 0)
    for c in range(CHUNKS):
        whole(picks.at[c], one_send.at[c]).wait()
        whole(send.at[c, pl.ds(0, n - 1)], two_send.at[c]).wait()
        pltpu.make_async_copy(send.at[c, me], got_ref.at[c, me], local_sem.at[c]).wait()
        whole(got_ref.at[c, pl.ds(0, n - 1)], two_recv.at[c]).wait()


def finish_kernel(
    pieces, pairs_in, got_ref, member_ref, table_ref, new_ref, gram_ref, pairs_ref, newv, sems
):
    me = lax.axis_index("ingest")
    book = lax.axis_index("codes")
    first_row = book * KB + me * pieces
    other_start = (1 - book) * KB
    load = pltpu.make_async_copy(pairs_in, pairs_ref, sems.at[0])
    load.start()
    f32 = jnp.float32
    member = member_ref[...]
    load.wait()

    for piece in range(pieces):

        def place(p, carry):
            block = pairs_ref[first_row + piece, p] - other_start
            pltpu.make_async_copy(
                table_ref.at[block, pl.ds(piece * BLK, BLK)],
                gram_ref.at[0, pl.ds(piece * BLK, BLK), pl.ds(pl.multiple_of(p * BLK, BLK), BLK)],
                sems.at[1],
            ).start()
            return carry

        lax.fori_loop(0, P_SIZE, place, 0)

    count = jnp.sum(member.astype(f32), axis=1, keepdims=True)
    scale = 1.0 / (count + 2.0)
    slots = member.shape[1]
    width = got_ref.shape[-1]
    for c in range(CHUNKS):
        rows_in = got_ref[c].reshape(slots, width)
        total = jnp.dot(member, rows_in, preferred_element_type=f32)
        newv[0, :, c * width : (c + 1) * width] = total * scale
    store = pltpu.make_async_copy(newv, new_ref, sems.at[0])
    store.start()
    store.wait()
    whole(gram_ref, sems.at[1]).wait()


def two_books(vectors, codes, codebook, pairs):
    n = lax.axis_size("ingest")
    rows, dim = vectors.shape
    own = codebook.shape[1]
    cap = 2 * rows // n
    slots = n * cap
    width = dim // CHUNKS
    f32, bf16 = jnp.float32, jnp.bfloat16
    vmem = pl.BlockSpec(memory_space=pltpu.VMEM)
    hbm = pl.BlockSpec(memory_space=pltpu.HBM)
    dma = pltpu.SemaphoreType.DMA
    block = (CHUNKS, n, cap, width)
    got, table, member, pairs = pl.pallas_call(
        functools.partial(exchange_kernel, n, own, cap),
        out_shape=(
            jax.ShapeDtypeStruct(block, bf16),
            jax.ShapeDtypeStruct((KB, own, BLK), f32),
            jax.ShapeDtypeStruct((own, slots), bf16),
            jax.ShapeDtypeStruct(pairs.shape, jnp.int32),
        ),
        in_specs=[hbm] * 4,
        out_specs=(vmem,) * 4,
        scratch_shapes=[
            pltpu.VMEM(codes.shape, jnp.int32),
            pltpu.VMEM((rows, dim), bf16),
            pltpu.VMEM((own, dim), bf16),
            pltpu.VMEM((n,) + codes.shape, jnp.int32),
            pltpu.VMEM(block, bf16),
            pltpu.VMEM(block, bf16),
            pltpu.VMEM(block, bf16),
            dma((n,)),
            dma((n,)),
            dma((CHUNKS,)),
            dma((CHUNKS,)),
            dma((CHUNKS,)),
            dma((CHUNKS,)),
            dma((CHUNKS,)),
            dma((4,)),
        ],
        compiler_params=pltpu.CompilerParams(
            collective_id=0, has_side_effects=True, vmem_limit_bytes=VMEM_BYTES
        ),
        name="exchange",
    )(*(pltpu.with_memory_space_constraint(a, pltpu.HBM) for a in (codes, vectors, codebook[0], pairs)))
    return pl.pallas_call(
        functools.partial(finish_kernel, own // BLK),
        out_shape=(
            jax.ShapeDtypeStruct((1, own, dim), f32),
            jax.ShapeDtypeStruct((1, own, P_SIZE * BLK), f32),
        ),
        in_specs=[vmem] * 4,
        out_specs=(hbm, hbm),
        scratch_shapes=[
            pltpu.SMEM(pairs.shape, jnp.int32),
            pltpu.VMEM((1, own, dim), f32),
            dma((2,)),
        ],
        compiler_params=pltpu.CompilerParams(vmem_limit_bytes=16 * 1024 * 1024),
        name="finish",
    )(pairs, got, member, table)


def shards(vectors, codes, codebook, pairs):
    owners = lax.axis_size("ingest")
    my_owner = lax.axis_index("ingest")
    my_group = lax.axis_index("codes")
    rows_count = vectors.shape[0]
    books_dev = codebook.shape[0]
    own_rows = codebook.shape[1]
    feature_dim = codebook.shape[2]
    codebooks = codes.shape[0]
    capacity = 2 * rows_count // owners
    slot_total = owners * books_dev * capacity
    local_codes = lax.dynamic_slice_in_dim(codes, my_group * books_dev, books_dev, 0)
    target = local_codes // own_rows
    within = local_codes - target * own_rows
    owner_hits = (target[:, :, None] == jnp.arange(owners, dtype=jnp.int32)).astype(jnp.int32)
    before = jnp.cumsum(owner_hits, axis=1) - owner_hits
    slot_rank = jnp.sum(before * owner_hits, axis=2)
    book_offset = jnp.arange(books_dev, dtype=jnp.int32)[:, None]
    slot_index = (target * books_dev + book_offset) * capacity + slot_rank
    slot_flat = slot_index.reshape(-1)
    vector_ids = jnp.broadcast_to(
        jnp.arange(rows_count, dtype=jnp.int32), (books_dev, rows_count)
    ).reshape(-1)
    slot_vector = jnp.full((slot_total,), rows_count, jnp.int32).at[slot_flat].set(vector_ids)
    asked_rows = (within + book_offset * own_rows).reshape(-1)
    slot_request = jnp.full((slot_total,), -1, jnp.int32).at[slot_flat].set(asked_rows)
    slot_request = slot_request.reshape(owners, books_dev * capacity)
    flat_book = codebook.reshape(books_dev * own_rows, feature_dim)
    picked = jnp.take(
        flat_book,
        jnp.maximum(
            lax.all_to_all(slot_request, "ingest", split_axis=0, concat_axis=0, tiled=True), 0
        ),
        axis=0,
    )
    returned = lax.all_to_all(picked, "ingest", split_axis=0, concat_axis=0, tiled=True)
    fetched = jnp.take(returned.reshape(slot_total, feature_dim), slot_index, axis=0)
    partial_sum = jnp.sum(fetched.astype(jnp.float32), axis=0)
    full_sum = lax.psum(partial_sum.astype(jnp.bfloat16), "codes").astype(jnp.float32)
    residual = (vectors.astype(jnp.float32) - full_sum).astype(jnp.bfloat16)
    residual_ext = jnp.concatenate([residual, jnp.zeros((1, feature_dim), jnp.bfloat16)], axis=0)
    codes_ext = jnp.concatenate([codes.T, jnp.full((1, codebooks), -1, jnp.int32)], axis=0)
    send_rows = jnp.take(residual_ext, slot_vector, axis=0).reshape(
        owners, books_dev * capacity, feature_dim
    )
    send_codes = jnp.take(codes_ext, slot_vector, axis=0).reshape(
        owners, books_dev * capacity, codebooks
    )
    got_rows, got_codes = (
        lax.all_to_all(send_rows, "ingest", split_axis=0, concat_axis=0, tiled=True),
        lax.all_to_all(send_codes, "ingest", split_axis=0, concat_axis=0, tiled=True),
    )
    got_rows = got_rows.reshape(owners, books_dev, capacity, feature_dim)
    got_codes = got_codes.reshape(owners, books_dev, capacity, codebooks)
    block_rows = min(own_rows, BLK)
    pieces = own_rows // block_rows
    group_size = min(P_SIZE, 8)
    contract = (((0,), (0,)), ((), ()))
    rows_in = got_rows[:, 0].reshape(owners * capacity, feature_dim)
    tuples = got_codes[:, 0].reshape(owners * capacity, codebooks)
    book_global = my_group * books_dev + 0
    own_code = lax.dynamic_index_in_dim(tuples, book_global, 1, keepdims=False)
    local_row = own_code - my_owner * own_rows
    member = (local_row[:, None] == jnp.arange(own_rows, dtype=jnp.int32)).astype(jnp.bfloat16)
    right_side = lax.dot_general(member, rows_in, contract, preferred_element_type=jnp.float32)
    code_count = jnp.sum(member, axis=0, dtype=jnp.float32)
    current = codebook[0].astype(jnp.float32)
    updated_list = [current + (right_side - 2.0 * current) / (code_count[:, None] + 2.0)]
    gram_pieces = []
    for part_index in range(pieces):
        first_row = book_global * K + my_owner * own_rows + part_index * block_rows
        partner = lax.dynamic_index_in_dim(pairs, first_row // BLK, 0, keepdims=False)
        partner_book = partner // KB
        partner_start = partner % KB * BLK
        partner_code = jnp.take(tuples, partner_book, axis=1) - partner_start[None, :]
        member_part = member[:, part_index * block_rows : (part_index + 1) * block_rows]
        columns = []
        for group_index in range(P_SIZE // group_size):
            chosen = partner_code[:, group_index * group_size : (group_index + 1) * group_size]
            onehot_table = (chosen[:, :, None] == jnp.arange(BLK, dtype=jnp.int32)).astype(
                jnp.bfloat16
            )
            onehot_table = onehot_table.reshape(chosen.shape[0], group_size * BLK)
            columns.append(
                lax.dot_general(
                    member_part, onehot_table, contract, preferred_element_type=jnp.float32
                )
            )
        gram_pieces.append(jnp.concatenate(columns, axis=1))
    gram_list = [jnp.concatenate(gram_pieces, axis=0)]
    return (jnp.stack(updated_list), jnp.stack(gram_list))


def solution(mesh):
    in_specs = (P("ingest", None), P(None, "ingest"), P("codes", "ingest", None), P())
    out_specs = (P("codes", "ingest", None), P("codes", "ingest", None))
    part = two_books if mesh.shape["codes"] == 2 else shards
    return jax.shard_map(part, mesh=mesh, in_specs=in_specs, out_specs=out_specs, check_vma=False)
```

```python
import functools

import jax
import jax.numpy as jnp
from jax import lax
from jax.experimental import pallas as pl
from jax.experimental.pallas import tpu as pltpu
from jax.sharding import PartitionSpec as P

K = 4096
BLK = 128
P_SIZE = 64
KB = 32
CHUNKS = 2
STORES = 8
MESH = pl.DeviceIdType.MESH
VMEM_BYTES = 32 * 1024 * 1024


def whole(ref, sem):
    return pltpu.make_async_copy(ref, ref, sem)


def exchange_kernel(
    n, own, cap,
    codes_hbm, vec_hbm, book_hbm, pairs_hbm,
    got_ref, blocks_ref, member_ref,
    codes_ref, vec_ref, book_ref, allc, picks, ret, send, table_ref, pairs_ref,
    code_send, code_recv, one_send, one_recv, two_send, two_recv, local_sem, in_sem,
):
    me = lax.axis_index("ingest")
    book = lax.axis_index("codes")
    other = 1 - book
    rows, dim = vec_ref.shape
    width = dim // CHUNKS
    slots = n * cap
    f32, bf16, i32 = jnp.float32, jnp.bfloat16, jnp.int32

    load_codes = pltpu.make_async_copy(codes_hbm, codes_ref, in_sem.at[0])
    load_codes.start()
    load_book = pltpu.make_async_copy(book_hbm, book_ref, in_sem.at[1])
    load_book.start()
    load_vectors = pltpu.make_async_copy(vec_hbm, vec_ref, in_sem.at[2])
    load_vectors.start()
    load_pairs = pltpu.make_async_copy(pairs_hbm, pairs_ref, in_sem.at[3])
    load_pairs.start()

    barrier = pltpu.get_barrier_semaphore()

    def greet(step, carry):
        peer = lax.rem(me + step, n)
        pl.semaphore_signal(barrier, inc=1, device_id=(peer, book), device_id_type=MESH)
        pl.semaphore_signal(barrier, inc=1, device_id=(peer, other), device_id_type=MESH)
        return carry

    pl.semaphore_signal(barrier, inc=1, device_id=(me, other), device_id_type=MESH)
    lax.fori_loop(1, n, greet, 0)
    load_codes.wait()
    pl.semaphore_wait(barrier, 2 * n - 1)

    def code_copy(step):
        peer = lax.rem(me + step, n)
        return pltpu.make_async_remote_copy(
            src_ref=codes_ref,
            dst_ref=allc.at[me],
            send_sem=code_send.at[step],
            recv_sem=code_recv.at[me],
            device_id=(peer, book),
            device_id_type=MESH,
        )

    def start_codes(step, carry):
        code_copy(step).start()
        return carry

    lax.fori_loop(1, n, start_codes, 0)

    earlier = (
        lax.broadcasted_iota(i32, (rows, rows), 0) < lax.broadcasted_iota(i32, (rows, rows), 1)
    ).astype(bf16)
    mine = codes_ref[...]
    first, second = mine[0:1, :], mine[1:2, :]
    own_code = jnp.where(book == 0, first, second)
    oth_code = jnp.where(book == 0, second, first)

    def slot_table(code):
        target = code // own
        hits = (target == lax.broadcasted_iota(i32, (n, rows), 0)).astype(f32)
        before = jnp.dot(hits.astype(bf16), earlier, preferred_element_type=f32)
        rank = jnp.sum(before * hits, axis=0, keepdims=True)
        slot = target * cap + rank.astype(i32)
        return (slot == lax.broadcasted_iota(i32, (slots, rows), 0)).astype(f32)

    send_table = slot_table(own_code).astype(bf16)
    merge_table = jnp.transpose(slot_table(oth_code)).astype(bf16)

    allc[me] = mine

    def wait_codes(step, carry):
        source = lax.rem(me + step, n)
        whole(allc.at[source], code_recv.at[source]).wait()
        return carry

    lax.fori_loop(1, n, wait_codes, 0)

    all_codes = allc[...]
    firsts, seconds = all_codes[:, 0, :], all_codes[:, 1, :]
    own_all = jnp.where(book == 0, firsts, seconds)
    oth_all = jnp.where(book == 0, seconds, firsts)
    local = own_all - me * own
    inside = (local >= 0) & (local < own)
    before = jnp.dot(
        jnp.where(inside, 1.0, 0.0).astype(bf16), earlier, preferred_element_type=f32
    )
    rank = jnp.where(inside, before, -1.0).astype(i32)
    chosen = rank[:, None, :] == lax.broadcasted_iota(i32, (n, cap, rows), 1)
    local_one = (local + 1).astype(f32)
    row_code = jnp.sum(jnp.where(chosen, local_one[:, None, :], 0.0), axis=2, keepdims=True)
    row_code = row_code.reshape(slots, 1).astype(i32) - 1
    member32 = (row_code == lax.broadcasted_iota(i32, (slots, own), 1)).astype(f32)
    member = member32.astype(bf16)

    load_book.wait()

    for c in range(CHUNKS):
        part = jnp.dot(
            member, book_ref[:, c * width : (c + 1) * width], preferred_element_type=f32
        )
        picks[c] = part.astype(bf16).reshape(n, cap, width)

        def start_one(step, carry):
            peer = lax.rem(me + step, n)
            pltpu.make_async_remote_copy(
                src_ref=picks.at[c, peer],
                dst_ref=ret.at[c, me],
                send_sem=one_send.at[c],
                recv_sem=one_recv.at[c],
                device_id=(peer, other),
                device_id_type=MESH,
            ).start()
            return carry

        lax.fori_loop(0, n, start_one, 0)

    load_vectors.wait()
    load_pairs.wait()

    for c in range(CHUNKS):
        whole(ret.at[c], one_recv.at[c]).wait()
        rows_in = ret[c].reshape(slots, width)
        fetched = jnp.dot(merge_table, rows_in, preferred_element_type=f32)
        target = vec_ref[:, c * width : (c + 1) * width].astype(f32) - fetched
        part = jnp.dot(send_table, target.astype(bf16), preferred_element_type=f32)
        send[c] = part.astype(bf16).reshape(n, cap, width)

        def start_two(step, carry):
            peer = lax.rem(me + step, n)
            pltpu.make_async_remote_copy(
                src_ref=send.at[c, peer],
                dst_ref=got_ref.at[c, me],
                send_sem=two_send.at[c],
                recv_sem=two_recv.at[c],
                device_id=(peer, book),
                device_id_type=MESH,
            ).start()
            return carry

        lax.fori_loop(1, n, start_two, 0)
        pltpu.make_async_copy(send.at[c, me], got_ref.at[c, me], local_sem.at[c]).start()

    oth_one = (oth_all + 1).astype(f32)
    oth_slot = jnp.sum(jnp.where(chosen, oth_one[:, None, :], 0.0), axis=2, keepdims=True)
    oth_slot = oth_slot.reshape(slots, 1).astype(i32) - 1
    member_ref[...] = jnp.transpose(member32).astype(bf16)
    group = 4

    def count_pairs(q, carry):
        columns = lax.broadcasted_iota(i32, (slots, group * BLK), 1) + q * (group * BLK)
        onehot = (oth_slot == columns).astype(f32).astype(bf16)
        counts = jnp.dot(member_ref[...], onehot, preferred_element_type=f32)
        for i in range(group):
            table_ref[q * group + i] = counts[:, i * BLK : (i + 1) * BLK]
        return carry

    lax.fori_loop(0, KB // group, count_pairs, 0)

    pieces = own // BLK
    for piece in range(pieces):
        piece_rows = pl.ds(piece * BLK, BLK)

        def put(p, carry):
            block = pairs_ref[book * KB + me * pieces + piece, p] % KB
            columns = pl.ds(pl.multiple_of(p * BLK, BLK), BLK)
            blocks_ref[piece_rows, columns] = table_ref[block, piece_rows]
            return carry

        lax.fori_loop(0, P_SIZE, put, 0)

    def wait_code_sends(step, carry):
        code_copy(step).wait_send()
        return carry

    lax.fori_loop(1, n, wait_code_sends, 0)
    for c in range(CHUNKS):
        whole(picks.at[c], one_send.at[c]).wait()
        whole(send.at[c, pl.ds(0, n - 1)], two_send.at[c]).wait()
        pltpu.make_async_copy(send.at[c, me], got_ref.at[c, me], local_sem.at[c]).wait()
        whole(got_ref.at[c, pl.ds(0, n - 1)], two_recv.at[c]).wait()


def finish_kernel(got_ref, member_ref, blocks_ref, new_ref, gram_ref, newv, sems):
    f32 = jnp.float32
    own = member_ref.shape[0]
    for part in range(STORES):
        part_rows = pl.ds(part * (own // STORES), own // STORES)
        pltpu.make_async_copy(
            blocks_ref.at[part_rows], gram_ref.at[0, part_rows], sems.at[1]
        ).start()
    member = member_ref[...]
    count = jnp.sum(member.astype(f32), axis=1, keepdims=True)
    scale = 1.0 / (count + 2.0)
    slots = member.shape[1]
    width = got_ref.shape[-1]
    for c in range(CHUNKS):
        rows_in = got_ref[c].reshape(slots, width)
        total = jnp.dot(member, rows_in, preferred_element_type=f32)
        newv[0, :, c * width : (c + 1) * width] = total * scale
    store = pltpu.make_async_copy(newv, new_ref, sems.at[0])
    store.start()
    store.wait()
    whole(blocks_ref, sems.at[1]).wait()


def two_books(vectors, codes, codebook, pairs):
    n = lax.axis_size("ingest")
    rows, dim = vectors.shape
    own = codebook.shape[1]
    cap = 2 * rows // n
    slots = n * cap
    width = dim // CHUNKS
    f32, bf16 = jnp.float32, jnp.bfloat16
    vmem = pl.BlockSpec(memory_space=pltpu.VMEM)
    hbm = pl.BlockSpec(memory_space=pltpu.HBM)
    dma = pltpu.SemaphoreType.DMA
    block = (CHUNKS, n, cap, width)
    got, blocks, member = pl.pallas_call(
        functools.partial(exchange_kernel, n, own, cap),
        out_shape=(
            jax.ShapeDtypeStruct(block, bf16),
            jax.ShapeDtypeStruct((own, P_SIZE * BLK), f32),
            jax.ShapeDtypeStruct((own, slots), bf16),
        ),
        in_specs=[hbm] * 4,
        out_specs=(vmem,) * 3,
        scratch_shapes=[
            pltpu.VMEM(codes.shape, jnp.int32),
            pltpu.VMEM((rows, dim), bf16),
            pltpu.VMEM((own, dim), bf16),
            pltpu.VMEM((n,) + codes.shape, jnp.int32),
            pltpu.VMEM(block, bf16),
            pltpu.VMEM(block, bf16),
            pltpu.VMEM(block, bf16),
            pltpu.VMEM((KB, own, BLK), f32),
            pltpu.SMEM(pairs.shape, jnp.int32),
            dma((n,)),
            dma((n,)),
            dma((CHUNKS,)),
            dma((CHUNKS,)),
            dma((CHUNKS,)),
            dma((CHUNKS,)),
            dma((CHUNKS,)),
            dma((4,)),
        ],
        compiler_params=pltpu.CompilerParams(
            collective_id=0, has_side_effects=True, vmem_limit_bytes=VMEM_BYTES
        ),
        name="exchange",
    )(*(pltpu.with_memory_space_constraint(a, pltpu.HBM) for a in (codes, vectors, codebook[0], pairs)))
    return pl.pallas_call(
        finish_kernel,
        out_shape=(
            jax.ShapeDtypeStruct((1, own, dim), f32),
            jax.ShapeDtypeStruct((1, own, P_SIZE * BLK), f32),
        ),
        in_specs=[vmem] * 3,
        out_specs=(hbm, hbm),
        scratch_shapes=[
            pltpu.VMEM((1, own, dim), f32),
            dma((2,)),
        ],
        compiler_params=pltpu.CompilerParams(vmem_limit_bytes=16 * 1024 * 1024),
        name="finish",
    )(got, member, blocks)


def shards(vectors, codes, codebook, pairs):
    owners = lax.axis_size("ingest")
    my_owner = lax.axis_index("ingest")
    my_group = lax.axis_index("codes")
    rows_count = vectors.shape[0]
    books_dev = codebook.shape[0]
    own_rows = codebook.shape[1]
    feature_dim = codebook.shape[2]
    codebooks = codes.shape[0]
    capacity = 2 * rows_count // owners
    slot_total = owners * books_dev * capacity
    local_codes = lax.dynamic_slice_in_dim(codes, my_group * books_dev, books_dev, 0)
    target = local_codes // own_rows
    within = local_codes - target * own_rows
    owner_hits = (target[:, :, None] == jnp.arange(owners, dtype=jnp.int32)).astype(jnp.int32)
    before = jnp.cumsum(owner_hits, axis=1) - owner_hits
    slot_rank = jnp.sum(before * owner_hits, axis=2)
    book_offset = jnp.arange(books_dev, dtype=jnp.int32)[:, None]
    slot_index = (target * books_dev + book_offset) * capacity + slot_rank
    slot_flat = slot_index.reshape(-1)
    vector_ids = jnp.broadcast_to(
        jnp.arange(rows_count, dtype=jnp.int32), (books_dev, rows_count)
    ).reshape(-1)
    slot_vector = jnp.full((slot_total,), rows_count, jnp.int32).at[slot_flat].set(vector_ids)
    asked_rows = (within + book_offset * own_rows).reshape(-1)
    slot_request = jnp.full((slot_total,), -1, jnp.int32).at[slot_flat].set(asked_rows)
    slot_request = slot_request.reshape(owners, books_dev * capacity)
    flat_book = codebook.reshape(books_dev * own_rows, feature_dim)
    picked = jnp.take(
        flat_book,
        jnp.maximum(
            lax.all_to_all(slot_request, "ingest", split_axis=0, concat_axis=0, tiled=True), 0
        ),
        axis=0,
    )
    returned = lax.all_to_all(picked, "ingest", split_axis=0, concat_axis=0, tiled=True)
    fetched = jnp.take(returned.reshape(slot_total, feature_dim), slot_index, axis=0)
    partial_sum = jnp.sum(fetched.astype(jnp.float32), axis=0)
    full_sum = lax.psum(partial_sum.astype(jnp.bfloat16), "codes").astype(jnp.float32)
    residual = (vectors.astype(jnp.float32) - full_sum).astype(jnp.bfloat16)
    residual_ext = jnp.concatenate([residual, jnp.zeros((1, feature_dim), jnp.bfloat16)], axis=0)
    codes_ext = jnp.concatenate([codes.T, jnp.full((1, codebooks), -1, jnp.int32)], axis=0)
    send_rows = jnp.take(residual_ext, slot_vector, axis=0).reshape(
        owners, books_dev * capacity, feature_dim
    )
    send_codes = jnp.take(codes_ext, slot_vector, axis=0).reshape(
        owners, books_dev * capacity, codebooks
    )
    got_rows, got_codes = (
        lax.all_to_all(send_rows, "ingest", split_axis=0, concat_axis=0, tiled=True),
        lax.all_to_all(send_codes, "ingest", split_axis=0, concat_axis=0, tiled=True),
    )
    got_rows = got_rows.reshape(owners, books_dev, capacity, feature_dim)
    got_codes = got_codes.reshape(owners, books_dev, capacity, codebooks)
    block_rows = min(own_rows, BLK)
    pieces = own_rows // block_rows
    group_size = min(P_SIZE, 8)
    contract = (((0,), (0,)), ((), ()))
    rows_in = got_rows[:, 0].reshape(owners * capacity, feature_dim)
    tuples = got_codes[:, 0].reshape(owners * capacity, codebooks)
    book_global = my_group * books_dev + 0
    own_code = lax.dynamic_index_in_dim(tuples, book_global, 1, keepdims=False)
    local_row = own_code - my_owner * own_rows
    member = (local_row[:, None] == jnp.arange(own_rows, dtype=jnp.int32)).astype(jnp.bfloat16)
    right_side = lax.dot_general(member, rows_in, contract, preferred_element_type=jnp.float32)
    code_count = jnp.sum(member, axis=0, dtype=jnp.float32)
    current = codebook[0].astype(jnp.float32)
    updated_list = [current + (right_side - 2.0 * current) / (code_count[:, None] + 2.0)]
    gram_pieces = []
    for part_index in range(pieces):
        first_row = book_global * K + my_owner * own_rows + part_index * block_rows
        partner = lax.dynamic_index_in_dim(pairs, first_row // BLK, 0, keepdims=False)
        partner_book = partner // KB
        partner_start = partner % KB * BLK
        partner_code = jnp.take(tuples, partner_book, axis=1) - partner_start[None, :]
        member_part = member[:, part_index * block_rows : (part_index + 1) * block_rows]
        columns = []
        for group_index in range(P_SIZE // group_size):
            chosen = partner_code[:, group_index * group_size : (group_index + 1) * group_size]
            onehot_table = (chosen[:, :, None] == jnp.arange(BLK, dtype=jnp.int32)).astype(
                jnp.bfloat16
            )
            onehot_table = onehot_table.reshape(chosen.shape[0], group_size * BLK)
            columns.append(
                lax.dot_general(
                    member_part, onehot_table, contract, preferred_element_type=jnp.float32
                )
            )
        gram_pieces.append(jnp.concatenate(columns, axis=1))
    gram_list = [jnp.concatenate(gram_pieces, axis=0)]
    return (jnp.stack(updated_list), jnp.stack(gram_list))


def solution(mesh):
    in_specs = (P("ingest", None), P(None, "ingest"), P("codes", "ingest", None), P())
    out_specs = (P("codes", "ingest", None), P("codes", "ingest", None))
    part = two_books if mesh.shape["codes"] == 2 else shards
    return jax.shard_map(part, mesh=mesh, in_specs=in_specs, out_specs=out_specs, check_vma=False)
```
